256 devices in a mesh: seq: 64 (over y_hi, z, x), chan: 4 (over y_lo, core).
Axes of the slice: x: 4, y: 4 (y_hi: 2, y_lo: 2; y = y_hi * 2 + y_lo), z: 8, core: 2. Of those that a mesh axis runs over, the one named last changes fastest.
Arguments:
- activation: bfloat16 [262144, 1024], P('seq', 'chan'), may hold values from -6 to 6
- gating: bfloat16 [262144, 1024], P('seq', 'chan'), may hold values from -6 to 6
- kernel_diag: bfloat16 [262144, 1024], P('seq', 'chan'), may hold values from -6 to 6
- cotangent: bfloat16 [262144, 1024], P('seq', 'chan'), may hold values from -6 to 6
- factor_right: bfloat16 [512, 512], replicated, may hold values from -0.25 to 0.25
- factor_left: bfloat16 [512, 512], replicated, may hold values from -0.25 to 0.25
- projection: bfloat16 [1024, 1024], P('chan'), may hold values from -0.1875 to 0.1875
Outputs:
- input_grad: bfloat16 [262144, 1024], P('seq', 'chan')
- projection_grad: float32 [1024, 1024], P('chan', 'seq')
- right_grad: float32 [512, 512], P('seq', 'chan')
- left_grad: float32 [512, 512], P('seq', 'chan')
The draws below stay inside these ranges and needn't reach their ends.
All inputs are finite; a program needn't handle non-finite values.
Results may differ from the reference program's by a relative error of at most 0.0064.
Values may be sent and summed in bfloat16 or wider, within the bound.
A program may use at most 128 MiB of HBM per device.

```python
import jax
import jax.numpy as jnp
from jax import lax

BLOCK = 512
WIDTH = 1024
POSITIONS = 262144


def levels(own_key, shape, split, low, high):
    level = 1.0
    for axis_at, shards_of in split:
        heights = jax.random.uniform(jax.random.fold_in(jax.random.fold_in(own_key, 6), axis_at), (shards_of,), jnp.float32, low / len(split), high / len(split))
        level = level * jnp.repeat(jnp.exp(heights), shape[axis_at] // shards_of).reshape((-1,) + (1,) * (len(shape) - 1 - axis_at))
    return level


def gaussian(own_key, extent, spread, reach, pieces=(), dtype=jnp.bfloat16):
    values = jax.random.normal(own_key, extent, jnp.float32) * spread
    if len(pieces) > 0:
        values = levels(own_key, extent, pieces, -0.22, 0.18) * values
    return jnp.clip(values, min=-reach, max=reach).astype(dtype)


def setup_inputs(seed: int = 0) -> dict:
    seeds = jax.random.split(jax.random.key(seed), 8)
    activation = gaussian(seeds[0], (POSITIONS, WIDTH), 1.0, 6.0, ((0, 64), (1, 4)))
    gating = gaussian(seeds[1], (POSITIONS, WIDTH), 1.0, 6.0, ((0, 64), (1, 4)))
    kernel_diag = gaussian(seeds[2], (POSITIONS, WIDTH), 1.0, 6.0, ((0, 64), (1, 4)))
    cotangent = gaussian(seeds[3], (POSITIONS, WIDTH), 1.0, 6.0, ((0, 64), (1, 4)))
    factor_right = gaussian(seeds[4], (BLOCK, BLOCK), BLOCK ** -0.5, 0.25)
    factor_left = gaussian(seeds[5], (BLOCK, BLOCK), BLOCK ** -0.5, 0.25)
    projection = gaussian(seeds[6], (WIDTH, WIDTH), WIDTH ** -0.5, 0.1875, ((0, 4),))
    return {"activation": activation, "gating": gating, "kernel_diag": kernel_diag, "cotangent": cotangent, "factor_right": factor_right, "factor_left": factor_left, "projection": projection}


GROUPING = 64


def rounded(value):
    return lax.optimization_barrier(value.astype(jnp.bfloat16)).astype(jnp.float32)


def regroup(array):
    return array.reshape(BLOCK, BLOCK, WIDTH // GROUPING, GROUPING).transpose(2, 0, 1, 3)


def ungroup(array):
    return array.transpose(1, 2, 0, 3).reshape(BLOCK * BLOCK, WIDTH)


def reference(activation, gating, kernel_diag, cotangent, factor_right, factor_left, projection):
    right_full = factor_right.astype(jnp.float32)
    left_full = factor_left.astype(jnp.float32)
    mixed_grad = jnp.dot(cotangent, projection.T, preferred_element_type=jnp.float32).astype(jnp.bfloat16)

    def per_group(operands):
        group_act, group_gate, group_kernel, group_grad = operands
        values = rounded(group_act.astype(jnp.float32) * group_gate.astype(jnp.float32))
        first_out = jnp.einsum("kj,ijd->ikd", right_full, values)
        scaled = rounded(first_out * group_kernel.astype(jnp.float32))
        mixed_out = jnp.einsum("mi,ikd->kmd", left_full, scaled).astype(jnp.bfloat16)
        upstream = group_grad.astype(jnp.float32)
        left_part = jnp.einsum("kmd,ikd->mi", upstream, scaled)
        scaled_grad = rounded(jnp.einsum("mi,kmd->ikd", left_full, upstream))
        first_grad = rounded(scaled_grad * group_kernel.astype(jnp.float32))
        right_part = jnp.einsum("ikd,ijd->kj", first_grad, values)
        values_grad = jnp.einsum("kj,ikd->ijd", right_full, first_grad)
        input_part = (values_grad * group_gate.astype(jnp.float32)).astype(jnp.bfloat16)
        return mixed_out, input_part, right_part, left_part

    mixed_out, input_part, right_parts, left_parts = lax.map(
        per_group, (regroup(activation), regroup(gating), regroup(kernel_diag), regroup(mixed_grad)))
    mixed_full = ungroup(mixed_out)
    projection_grad = jnp.dot(mixed_full.T, cotangent, preferred_element_type=jnp.float32) / BLOCK
    grad_scale = (BLOCK * WIDTH) ** -0.5
    right_grad = jnp.sum(right_parts, axis=0) * grad_scale
    left_grad = jnp.sum(left_parts, axis=0) * grad_scale
    return ungroup(input_part), projection_grad, right_grad, left_grad
```

```python
import jax
import jax.numpy as jnp
from jax import lax
from jax.sharding import PartitionSpec as P


def on_device(activation, gating, kernel_diag, cotangent, factor_right, factor_left, projection):
    row_count, chan_count = activation.shape
    block_size = factor_right.shape[0]
    local_blocks = row_count // block_size
    full_width = projection.shape[1]
    seq_size = lax.axis_size("seq")
    chan_size = lax.axis_size("chan")
    cube_shape = (local_blocks, block_size, chan_count)
    my_chan = lax.axis_index("chan")

    def swap(array, bit):
        return lax.ppermute(array, "chan", [(c, c ^ bit) for c in range(chan_size)])

    from_far = swap(cotangent, 2)
    from_sibling = swap(cotangent, 1)
    from_far_sibling = swap(from_far, 1)
    pieces = (cotangent, from_sibling, from_far, from_far_sibling)

    values = (
        (activation.astype(jnp.float32) * gating.astype(jnp.float32))
        .astype(jnp.bfloat16)
        .reshape(cube_shape)
    )
    kernel_cube = kernel_diag.astype(jnp.float32).reshape(cube_shape)
    first_out = jnp.einsum("kj,ijd->ikd", factor_right, values, preferred_element_type=jnp.float32)
    scaled = (first_out * kernel_cube).astype(jnp.bfloat16)
    received = lax.all_to_all(scaled, "seq", split_axis=1, concat_axis=0, tiled=True)

    order = my_chan ^ jnp.arange(chan_size)
    proj_blocks = projection.reshape(chan_count, chan_size, chan_count)
    proj_mine = jnp.take(proj_blocks, order, axis=1).reshape(chan_count, full_width)
    portion = jnp.concatenate(pieces, axis=1)
    grad_total = lax.dot_general(
        portion, proj_mine, (((1,), (1,)), ((), ())), preferred_element_type=jnp.float32
    )
    upstream = grad_total.astype(jnp.bfloat16).reshape(cube_shape)
    scaled_grad_out = jnp.einsum(
        "mi,kmd->ikd", factor_left, upstream, preferred_element_type=jnp.float32
    ).astype(jnp.bfloat16)
    scaled_grad = lax.all_to_all(scaled_grad_out, "seq", split_axis=0, concat_axis=1, tiled=True)

    mixed_flat = (
        jnp.einsum("mi,ikd->kmd", factor_left, received, preferred_element_type=jnp.float32)
        .astype(jnp.bfloat16)
        .reshape(row_count, chan_count)
    )
    updated = lax.dot_general(
        mixed_flat, portion, (((0,), (0,)), ((), ())), preferred_element_type=jnp.float32
    )
    updated = jnp.take(
        updated.reshape(chan_count, chan_size, chan_count), order, axis=1
    ).reshape(chan_count, full_width)
    left_part = jnp.einsum("kmd,ikd->mi", upstream, received, preferred_element_type=jnp.float32)

    first_grad = (scaled_grad.astype(jnp.float32) * kernel_cube).astype(jnp.bfloat16)
    right_part = jnp.einsum("ikd,ijd->kj", first_grad, values, preferred_element_type=jnp.float32)
    values_grad = jnp.einsum(
        "kj,ikd->ijd", factor_right, first_grad, preferred_element_type=jnp.float32
    )
    input_grad = (
        (values_grad * gating.astype(jnp.float32).reshape(cube_shape))
        .astype(jnp.bfloat16)
        .reshape(row_count, chan_count)
    )

    grad_scale = (block_size * full_width) ** (-0.5)
    row_share = block_size // seq_size
    col_share = block_size // chan_size
    out_share = full_width // seq_size

    def over_chan(part):
        blocks = part.astype(jnp.bfloat16).reshape(block_size, chan_size, col_share)
        blocks = blocks.transpose(1, 0, 2)
        arrived = lax.all_to_all(blocks, "chan", split_axis=0, concat_axis=0, tiled=True)
        return jnp.sum(arrived.astype(jnp.float32), axis=0)

    def over_seq(blocks):
        arrived = lax.all_to_all(
            blocks.astype(jnp.bfloat16), "seq", split_axis=0, concat_axis=0, tiled=True
        )
        return jnp.sum(arrived.astype(jnp.float32), axis=0)

    proj_rows = updated.reshape(chan_count, seq_size, out_share).transpose(1, 0, 2)
    proj_rows = proj_rows.reshape(seq_size, -1, col_share)
    left_rows = over_chan(left_part).reshape(seq_size, row_share, col_share)
    early = over_seq(jnp.concatenate([proj_rows, left_rows], axis=1))
    proj_count = proj_rows.shape[1]
    projection_grad = early[:proj_count].reshape(chan_count, out_share) / block_size
    left_grad = early[proj_count:] * grad_scale
    right_rows = over_chan(right_part).reshape(seq_size, row_share, col_share)
    right_grad = over_seq(right_rows) * grad_scale
    return (input_grad, projection_grad, right_grad, left_grad)


def solution(mesh):
    in_specs = (
        P("seq", "chan"),
        P("seq", "chan"),
        P("seq", "chan"),
        P("seq", "chan"),
        P(),
        P(),
        P("chan", None),
    )
    out_specs = (P("seq", "chan"), P("chan", "seq"), P("seq", "chan"), P("seq", "chan"))
    return jax.shard_map(
        on_device, mesh=mesh, in_specs=in_specs, out_specs=out_specs, check_vma=False
    )
```

```python
import functools

import jax
import jax.numpy as jnp
from jax import lax
from jax.experimental import pallas as pl
from jax.experimental.pallas import tpu as pltpu
from jax.sharding import PartitionSpec as P

ROUNDS = 4
LANES = 128
F32 = jnp.float32
BF16 = jnp.bfloat16


def matmul(left, right):
    return jnp.dot(left, right, preferred_element_type=F32)


def matmul_nt(left, right):
    return lax.dot_general(left, right, (((1,), (1,)), ((), ())), preferred_element_type=F32)


def kernel(
    scale,
    act_hbm, gate_hbm, diag_hbm, cot_hbm, right_hbm, left_hbm, proj_hbm,
    input_grad_hbm, proj_grad_ref, right_grad_ref, left_grad_ref,
    act, gate, diag, cot, fr, fl, proj, frt, flt,
    vals, send1, recv1, mg, send2, recv2, staging, out,
    p_acc, p_send, p_recv,
    l_acc, l_send, l_recv, l2_send, l2_recv,
    r_send, r_recv, r2_send, r2_recv,
    in_sem, out_sem,
    far_send, far_recv, sib_send, sib_recv, fwd_send, fwd_recv,
    s1_send, s1_recv, s2_send, s2_recv,
    p_ssem, p_rsem, l_ssem, l_rsem, l2_ssem, l2_rsem, r_ssem, r_rsem, r2_ssem, r2_rsem,
):
    seq_size = recv1.shape[0]
    lb, block, width = vals.shape
    per_round = lb // ROUNDS
    rows = per_round * lb
    chans = cot.shape[0]
    me = lax.axis_index("seq")
    mc = lax.axis_index("chan")
    sibling = mc + 1 - 2 * lax.rem(mc, 2)
    far = lax.rem(mc + 2, 4)
    far_sibling = 3 - mc

    barrier = pltpu.get_barrier_semaphore()

    def greet(step, carry):
        other = lax.rem(me + step, seq_size)
        pl.semaphore_signal(
            barrier, inc=1, device_id=(other, mc), device_id_type=pl.DeviceIdType.MESH
        )
        return carry

    for other in (sibling, far, far_sibling):
        pl.semaphore_signal(
            barrier, inc=1, device_id=(me, other), device_id_type=pl.DeviceIdType.MESH
        )
    lax.fori_loop(1, seq_size, greet, 0)

    loads = [
        pltpu.make_async_copy(src, dst, in_sem.at[at])
        for at, (src, dst) in enumerate(
            (
                (act_hbm, act),
                (gate_hbm, gate),
                (right_hbm, fr),
                (diag_hbm, diag),
                (cot_hbm, cot.at[mc]),
                (proj_hbm, proj),
                (left_hbm, fl),
            )
        )
    ]
    for load in loads:
        load.start()

    pl.semaphore_wait(barrier, seq_size - 1 + 3)

    def send(src, dst, send_sem, recv_sem, device):
        return pltpu.make_async_remote_copy(
            src_ref=src, dst_ref=dst, send_sem=send_sem, recv_sem=recv_sem,
            device_id=device, device_id_type=pl.DeviceIdType.MESH,
        )

    def drain(ref, sem):
        pltpu.make_async_copy(ref, ref, sem).wait()

    for turn in range(ROUNDS):
        part = pl.ds(turn * per_round, per_round)
        send(
            cot_hbm.at[part], cot.at[mc, part], far_send.at[turn], far_recv.at[turn], (me, far)
        ).start()
    for turn in range(ROUNDS):
        part = pl.ds(turn * per_round, per_round)
        send(
            cot_hbm.at[part], cot.at[mc, part], sib_send.at[turn], sib_recv.at[turn],
            (me, sibling),
        ).start()

    for load in loads[:4]:
        load.wait()

    def first_part(pair, carry):
        pieces = []
        for off in range(2):
            at = pair * 2 + off
            value = (act[at].astype(F32) * gate[at].astype(F32)).astype(BF16)
            vals[at] = value
            made = matmul(fr[...], value) * diag[at].astype(F32)
            pieces.append(made.reshape(seq_size, lb, width))
        send1[:, pl.ds(pl.multiple_of(pair * 2 * lb, 2 * lb), 2 * lb), :] = jnp.concatenate(
            pieces, axis=1
        ).astype(BF16)
        return carry

    lax.fori_loop(0, lb // 2, first_part, 0)

    def first_sends(step, carry):
        other = lax.rem(me + step, seq_size)
        send(send1.at[other], recv1.at[me], s1_send, s1_recv, (other, mc)).start()
        return carry

    lax.fori_loop(1, seq_size, first_sends, 0)
    recv1[me] = send1[me]

    for load in loads[4:]:
        load.wait()
    flt[...] = fl[...].T
    frt[...] = fr[...].T

    for turn in range(ROUNDS):
        part = pl.ds(turn * per_round, per_round)
        drain(cot.at[far, part], far_recv.at[turn])
        forward = send(
            cot.at[far, part], cot.at[far, part], fwd_send.at[turn], fwd_recv.at[turn],
            (me, sibling),
        )
        forward.start()
        drain(cot.at[sibling, part], sib_recv.at[turn])
        drain(cot.at[far_sibling, part], fwd_recv.at[turn])
        pieces = []
        for off in range(per_round):
            at = turn * per_round + off
            total = matmul_nt(cot[0, at], proj[:, :width])
            for c in range(1, chans):
                total += matmul_nt(cot[c, at], proj[:, c * width : (c + 1) * width])
            up = total.astype(BF16)
            mg[at] = up
            pieces.append(matmul(flt[...], up).reshape(seq_size, lb, width))
        send2[turn] = jnp.concatenate(pieces, axis=1).astype(BF16)

        def second_sends(step, carry, turn=turn):
            other = lax.rem(me + step, seq_size)
            send(
                send2.at[turn, other], recv2.at[me, turn], s2_send.at[turn], s2_recv.at[turn],
                (other, mc),
            ).start()
            return carry

        lax.fori_loop(1, seq_size, second_sends, 0)
        recv2[me, turn] = send2[turn, me]

    def stage(blocks):
        flat = blocks.reshape(block * lb, width).astype(F32)
        for part in range(width // LANES):
            staging[part] = flat[:, part * LANES : (part + 1) * LANES]

    def every(at):
        return jnp.concatenate(
            [
                staging[part, pl.ds(at, block, stride=lb), :]
                for part in range(width // LANES)
            ],
            axis=1,
        )

    drain(recv1.at[pl.ds(0, seq_size - 1)], s1_recv)
    stage(recv1[...])
    p_acc[...] = jnp.zeros_like(p_acc)
    l_acc[...] = jnp.zeros_like(l_acc)

    def mixed_part(at, carry):
        got = every(at).astype(BF16)
        l_acc[...] += matmul_nt(mg[at], got)
        mixed = matmul(fl[...], got).astype(BF16).T
        for c in range(chans):
            p_acc[:, c * width : (c + 1) * width] += matmul(mixed, cot[c, at])
        return carry

    lax.fori_loop(0, lb, mixed_part, 0)

    def over_chan(total, sends, recvs, ssem, rsem):
        share = block // chans
        for c in range(chans):
            sends[c] = total[:, c * share : (c + 1) * share].astype(BF16)
        for other in (far, far_sibling, sibling):
            send(sends.at[other], recvs.at[mc], ssem, rsem, (me, other)).start()
        recvs[mc] = sends[mc]

    def over_seq(recvs, rsem, sends2, recvs2, ssem2, rsem2):
        drain(recvs.at[pl.ds(0, chans - 1)], rsem)
        summed = recvs[0].astype(F32)
        for c in range(1, chans):
            summed += recvs[c].astype(F32)
        sends2[...] = summed.reshape(sends2.shape)

        def go(step, carry):
            other = lax.rem(me + step, seq_size)
            send(sends2.at[other], recvs2.at[me], ssem2, rsem2, (other, mc)).start()
            return carry

        lax.fori_loop(1, seq_size, go, 0)
        recvs2[me] = sends2[me]

    over_chan(l_acc, l_send, l_recv, l_ssem, l_rsem)
    share = p_send.shape[1]
    for c in range(chans):
        turned = p_acc[:, c * width : (c + 1) * width].T.astype(BF16)
        p_send[pl.ds(c * (width // share), width // share)] = turned.reshape(
            width // share, share, width
        )

    def proj_sends(step, carry):
        other = lax.rem(me + step, seq_size)
        send(p_send.at[other], p_recv.at[me], p_ssem, p_rsem, (other, mc)).start()
        return carry

    lax.fori_loop(1, seq_size, proj_sends, 0)
    p_recv[me] = p_send[me]
    over_seq(l_recv, l_rsem, l2_send, l2_recv, l2_ssem, l2_rsem)

    for turn in range(ROUNDS):
        drain(recv2.at[pl.ds(0, seq_size - 1), turn], s2_recv.at[turn])
    stage(recv2[...])
    l_acc[...] = jnp.zeros_like(l_acc)

    def right_part(at, carry):
        grad = (every(at) * diag[at].astype(F32)).astype(BF16)
        out[at] = grad
        l_acc[...] += matmul_nt(grad, vals[at])
        return carry

    lax.fori_loop(0, lb, right_part, 0)
    over_chan(l_acc, r_send, r_recv, r_ssem, r_rsem)

    def input_part(at, carry):
        out[at] = (matmul(frt[...], out[at]) * gate[at].astype(F32)).astype(BF16)
        return carry

    lax.fori_loop(0, lb, input_part, 0)
    store = pltpu.make_async_copy(out, input_grad_hbm, out_sem)
    store.start()
    over_seq(r_recv, r_rsem, r2_send, r2_recv, r2_ssem, r2_rsem)

    drain(p_recv.at[pl.ds(0, seq_size - 1)], p_rsem)
    proj_grad_ref[...] = jnp.sum(p_recv[...].astype(F32), axis=0) * (1.0 / block)
    drain(l2_recv.at[pl.ds(0, seq_size - 1)], l2_rsem)
    left_grad_ref[...] = jnp.sum(l2_recv[...], axis=0) * scale
    drain(r2_recv.at[pl.ds(0, seq_size - 1)], r2_rsem)
    right_grad_ref[...] = jnp.sum(r2_recv[...], axis=0) * scale

    store.wait()
    for turn in range(ROUNDS):
        part = pl.ds(turn * per_round, per_round)
        drain(cot.at[mc, part], far_send.at[turn])
        drain(cot.at[mc, part], sib_send.at[turn])
        drain(cot.at[far, part], fwd_send.at[turn])
        drain(send2.at[turn, pl.ds(0, seq_size - 1)], s2_send.at[turn])
    drain(send1.at[pl.ds(0, seq_size - 1)], s1_send)
    drain(p_send.at[pl.ds(0, seq_size - 1)], p_ssem)
    for sends, ssem, sends2, ssem2 in (
        (l_send, l_ssem, l2_send, l2_ssem),
        (r_send, r_ssem, r2_send, r2_ssem),
    ):
        drain(sends.at[pl.ds(0, chans - 1)], ssem)
        drain(sends2.at[pl.ds(0, seq_size - 1)], ssem2)


def on_device(activation, gating, kernel_diag, cotangent, factor_right, factor_left, projection):
    row_count, width = activation.shape
    block = factor_right.shape[0]
    lb = row_count // block
    full = projection.shape[1]
    seq_size = lax.axis_size("seq")
    chans = lax.axis_size("chan")
    cube = (lb, block, width)
    share = full // seq_size
    col = block // chans
    dma = pltpu.SemaphoreType.DMA
    per_round = lb // ROUNDS
    scratch = [
        pltpu.VMEM(cube, BF16),
        pltpu.VMEM(cube, BF16),
        pltpu.VMEM(cube, BF16),
        pltpu.VMEM((chans,) + cube, BF16),
        pltpu.VMEM((block, block), BF16),
        pltpu.VMEM((block, block), BF16),
        pltpu.VMEM((width, full), BF16),
        pltpu.VMEM((block, block), BF16),
        pltpu.VMEM((block, block), BF16),
        pltpu.VMEM(cube, BF16),
        pltpu.VMEM((seq_size, lb * lb, width), BF16),
        pltpu.VMEM((seq_size, lb * lb, width), BF16),
        pltpu.VMEM(cube, BF16),
        pltpu.VMEM((ROUNDS, seq_size, per_round * lb, width), BF16),
        pltpu.VMEM((seq_size, ROUNDS, per_round * lb, width), BF16),
        pltpu.VMEM((width // LANES, block * lb, LANES), F32),
        pltpu.VMEM(cube, BF16),
        pltpu.VMEM((width, full), F32),
        pltpu.VMEM((seq_size, share, width), BF16),
        pltpu.VMEM((seq_size, share, width), BF16),
        pltpu.VMEM((block, block), F32),
        pltpu.VMEM((chans, block, col), BF16),
        pltpu.VMEM((chans, block, col), BF16),
        pltpu.VMEM((seq_size, lb, col), F32),
        pltpu.VMEM((seq_size, lb, col), F32),
        pltpu.VMEM((chans, block, col), BF16),
        pltpu.VMEM((chans, block, col), BF16),
        pltpu.VMEM((seq_size, lb, col), F32),
        pltpu.VMEM((seq_size, lb, col), F32),
        dma((7,)), dma,
        dma((ROUNDS,)), dma((ROUNDS,)), dma((ROUNDS,)), dma((ROUNDS,)),
        dma((ROUNDS,)), dma((ROUNDS,)),
        dma, dma, dma((ROUNDS,)), dma((ROUNDS,)),
    ] + [dma] * 10
    any_space = pl.BlockSpec(memory_space=pl.ANY)
    vmem = pl.BlockSpec(memory_space=pltpu.VMEM)
    input_grad, proj_grad, right_grad, left_grad = pl.pallas_call(
        functools.partial(kernel, float((block * full) ** (-0.5))),
        out_shape=[
            jax.ShapeDtypeStruct(cube, BF16),
            jax.ShapeDtypeStruct((share, width), F32),
            jax.ShapeDtypeStruct((lb, col), F32),
            jax.ShapeDtypeStruct((lb, col), F32),
        ],
        in_specs=[any_space] * 7,
        out_specs=[any_space, vmem, vmem, vmem],
        scratch_shapes=scratch,
        compiler_params=pltpu.CompilerParams(
            collective_id=0, has_side_effects=True, vmem_limit_bytes=56 * 1024 * 1024
        ),
        cost_estimate=pl.CostEstimate(
            flops=20 * row_count * block * width, bytes_accessed=12 * row_count * width,
            transcendentals=0,
        ),
        name="monarch_backward",
    )(
        activation.reshape(cube), gating.reshape(cube), kernel_diag.reshape(cube),
        cotangent.reshape(cube), factor_right, factor_left, projection,
    )
    return (input_grad.reshape(row_count, width), proj_grad.T, right_grad, left_grad)


def solution(mesh):
    in_specs = (
        P("seq", "chan"),
        P("seq", "chan"),
        P("seq", "chan"),
        P("seq", "chan"),
        P(),
        P(),
        P("chan", None),
    )
    out_specs = (P("seq", "chan"), P("chan", "seq"), P("seq", "chan"), P("seq", "chan"))
    return jax.shard_map(
        on_device, mesh=mesh, in_specs=in_specs, out_specs=out_specs, check_vma=False
    )
```

```python
import functools

import jax
import jax.numpy as jnp
from jax import lax
from jax.experimental import pallas as pl
from jax.experimental.pallas import tpu as pltpu
from jax.sharding import PartitionSpec as P

ROUNDS = 4
LANES = 128
CROSS_AFTER = 2
F32 = jnp.float32
BF16 = jnp.bfloat16


def matmul(left, right):
    return jnp.dot(left, right, preferred_element_type=F32)


def matmul_nt(left, right):
    return lax.dot_general(left, right, (((1,), (1,)), ((), ())), preferred_element_type=F32)


def kernel(
    scale,
    act_hbm, gate_hbm, diag_hbm, cot_hbm, right_hbm, left_hbm, proj_hbm,
    input_grad_hbm, proj_grad_hbm, right_grad_hbm, left_grad_hbm,
    act, gate, diag, cot, fr, fl, proj, frt, flt, diag_turned,
    vals, send1, recv1, mg, send2, recv2, staging, out, out_acc,
    p_acc, p_send, p_xrecv, p_ysend, p_yrecv,
    l_acc, l_send, l_recv, l_ysend, l_yrecv,
    r_acc, r_send, r_recv, r_rows, r_ysend, r_yrecv,
    proj_grad, right_grad, left_grad,
    in_sem, out_sem, small_sem,
    far_send, far_recv, sib_send, sib_recv, fwd_send, fwd_recv,
    s1_send, s1_recv, s2_send, s2_recv, rg_send, rg_recv, lg_send, lg_recv,
    px_sems, py_sems, ly_sems, ry_sems,
):
    seq_size = recv1.shape[0]
    lb, block, width = vals.shape
    per_round = lb // ROUNDS
    rows = per_round * lb
    chans = cot.shape[0]
    me = lax.axis_index("seq")
    mc = lax.axis_index("chan")
    sibling = mc + 1 - 2 * lax.rem(mc, 2)
    far = lax.rem(mc + 2, 4)
    far_sibling = 3 - mc
    half = seq_size // 2
    xs = p_send.shape[0]
    zs = half // xs
    yzs = seq_size // xs
    my_half = me // half
    my_z = lax.rem(me, half) // xs
    my_x = lax.rem(me, xs)
    my_yz = me // xs

    barrier = pltpu.get_barrier_semaphore()

    def greet(step, carry):
        other = lax.rem(me + step, seq_size)
        pl.semaphore_signal(
            barrier, inc=1, device_id=(other, mc), device_id_type=pl.DeviceIdType.MESH
        )
        return carry

    group = [
        (x_off, lax.rem(my_x + x_off, xs), chan)
        for x_off in range(xs)
        for chan in (mc, sibling, far, far_sibling)
        if x_off > 0 or chan is not mc
    ]
    for x_off, x, chan in group:
        if chan is not mc:
            pl.semaphore_signal(
                barrier, inc=1, device_id=(my_yz * xs + x, chan),
                device_id_type=pl.DeviceIdType.MESH,
            )
    lax.fori_loop(1, seq_size, greet, 0)

    loads = [
        pltpu.make_async_copy(src, dst, in_sem.at[at])
        for at, (src, dst) in enumerate(
            (
                (act_hbm, act),
                (gate_hbm, gate),
                (right_hbm, fr),
                (diag_hbm, diag),
                (cot_hbm, cot.at[mc]),
                (proj_hbm, proj),
                (left_hbm, fl),
            )
        )
    ]
    for load in loads:
        load.start()

    pl.semaphore_wait(barrier, seq_size - 1 + xs * (chans - 1))

    def send(src, dst, send_sem, recv_sem, device):
        return pltpu.make_async_remote_copy(
            src_ref=src, dst_ref=dst, send_sem=send_sem, recv_sem=recv_sem,
            device_id=device, device_id_type=pl.DeviceIdType.MESH,
        )

    def drain(ref, sem):
        pltpu.make_async_copy(ref, ref, sem).wait()

    for turn in range(ROUNDS):
        part = pl.ds(turn * per_round, per_round)
        send(
            cot_hbm.at[part], cot.at[mc, part], far_send.at[turn], far_recv.at[turn], (me, far)
        ).start()
    for turn in range(ROUNDS):
        part = pl.ds(turn * per_round, per_round)
        send(
            cot_hbm.at[part], cot.at[mc, part], sib_send.at[turn], sib_recv.at[turn],
            (me, sibling),
        ).start()

    def place(step, cross):
        turn = lax.rem(step, zs)
        z_off = (2 * lax.rem(turn, 2) - 1) * ((turn + 1) // 2)
        x_off = step // zs
        z = lax.rem(my_z + z_off + zs, zs)
        x = lax.rem(my_x + x_off, xs)
        return lax.rem(my_half + cross, 2) * half + z * xs + x

    def first_sends(cross):
        def go(step, carry):
            other = place(step, cross)
            send(send1.at[other], recv1.at[me], s1_send, s1_recv, (other, mc)).start()
            return carry

        lax.fori_loop(1 - cross, half, go, 0)

    def second_sends(turn, cross):
        def go(step, carry):
            other = place(step, cross)
            send(
                send2.at[turn, other], recv2.at[me, turn], s2_send.at[turn], s2_recv.at[turn],
                (other, mc),
            ).start()
            return carry

        lax.fori_loop(1 - cross, half, go, 0)

    for load in loads[:4]:
        load.wait()

    def first_part(pair, carry):
        pieces = []
        for off in range(2):
            at = pair * 2 + off
            value = (act[at].astype(F32) * gate[at].astype(F32)).astype(BF16)
            vals[at] = value
            made = matmul(fr[...], value) * diag[at].astype(F32)
            pieces.append(made.reshape(seq_size, lb, width))
        send1[:, pl.ds(pl.multiple_of(pair * 2 * lb, 2 * lb), 2 * lb), :] = jnp.concatenate(
            pieces, axis=1
        ).astype(BF16)
        return carry

    lax.fori_loop(0, lb // 2, first_part, 0)
    first_sends(0)
    recv1[me] = send1[me]

    for load in loads[4:]:
        load.wait()
    flt[...] = fl[...].T

    def stage(blocks):
        count = blocks.shape[0] * blocks.shape[1]
        flat = blocks.reshape(count, width).astype(F32)
        for part in range(width // LANES):
            staging[part, :count] = flat[:, part * LANES : (part + 1) * LANES]

    def every(start, count, stride):
        return jnp.concatenate(
            [
                staging[part, pl.ds(start, count, stride=stride), :]
                for part in range(width // LANES)
            ],
            axis=1,
        )

    for col in range(block // LANES):
        staging[0, col * block : (col + 1) * block] = fr[
            :, col * LANES : (col + 1) * LANES
        ].astype(F32)
    for kk in range(lb):
        turned = jnp.concatenate(
            [
                staging[0, pl.ds(col * block + kk, seq_size, stride=lb), :]
                for col in range(block // LANES)
            ],
            axis=1,
        )
        frt[:, kk * seq_size : (kk + 1) * seq_size] = turned.T.astype(BF16)
    stage(diag[...])

    def turn_diag(kk, carry):
        diag_turned[kk] = every(kk, block, lb).astype(BF16)
        return carry

    lax.fori_loop(0, lb, turn_diag, 0)

    for turn in range(ROUNDS):
        part = pl.ds(turn * per_round, per_round)
        drain(cot.at[far, part], far_recv.at[turn])
        forward = send(
            cot.at[far, part], cot.at[far, part], fwd_send.at[turn], fwd_recv.at[turn],
            (me, sibling),
        )
        forward.start()
        drain(cot.at[sibling, part], sib_recv.at[turn])
        drain(cot.at[far_sibling, part], fwd_recv.at[turn])
        pieces = []
        for off in range(per_round):
            at = turn * per_round + off
            total = matmul_nt(cot[0, at], proj[:, :width])
            for c in range(1, chans):
                total += matmul_nt(cot[c, at], proj[:, c * width : (c + 1) * width])
            up = total.astype(BF16)
            mg[at] = up
            pieces.append(matmul(flt[...], up).reshape(seq_size, lb, width))
        send2[turn] = jnp.concatenate(pieces, axis=1).astype(BF16)
        second_sends(turn, 0)
        recv2[me, turn] = send2[turn, me]
        if turn == CROSS_AFTER:
            first_sends(1)
            for earlier in range(turn):
                second_sends(earlier, 1)
        if turn >= CROSS_AFTER:
            second_sends(turn, 1)

    drain(recv1.at[pl.ds(0, seq_size - 1)], s1_recv)
    stage(recv1[...])
    p_acc[...] = jnp.zeros_like(p_acc)
    l_acc[...] = jnp.zeros_like(l_acc)

    def mixed_part(at, carry):
        got = every(at, block, lb).astype(BF16)
        l_acc[...] += matmul_nt(mg[at], got)
        mixed = matmul(fl[...], got).astype(BF16).T
        for c in range(chans):
            p_acc[:, c * width : (c + 1) * width] += matmul(mixed, cot[c, at])
        return carry

    lax.fori_loop(0, lb, mixed_part, 0)

    def over_group(sends, recvs, ssem, rsem):
        mine = mc * xs + my_x
        for x_off, x, chan in group:
            send(
                sends.at[chan * xs + x], recvs.at[mine], ssem, rsem, (my_yz * xs + x, chan)
            ).start()
        recvs[mine] = sends[mine]

    def group_sum(recvs, rsem):
        drain(recvs.at[pl.ds(0, xs * chans - 1)], rsem)
        return jnp.sum(recvs[...].astype(F32), axis=0)

    def over_yz(total, sends, recvs, sems):
        sends[...] = total.astype(sends.dtype)

        def go(step, carry):
            other = lax.rem(my_yz + step, yzs)
            send(
                sends.at[other], recvs.at[my_yz], sems.at[0], sems.at[1],
                (other * xs + my_x, mc),
            ).start()
            return carry

        lax.fori_loop(1, yzs, go, 0)
        recvs[my_yz] = sends[my_yz]

    def yz_sum(recvs, sems):
        drain(recvs.at[pl.ds(0, yzs - 1)], sems.at[1])
        return jnp.sum(recvs[...].astype(F32), axis=0)

    col = block // chans
    split = l_acc[...].reshape(yzs, xs, lb, block)
    for c in range(chans):
        for x in range(xs):
            l_send[c * xs + x] = (
                split[:, x, :, c * col : (c + 1) * col].reshape(yzs * lb, col).astype(BF16)
            )
    over_group(l_send, l_recv, lg_send, lg_recv)
    share = p_send.shape[2]
    per_chan = yzs // chans
    for c in range(chans):
        turned = p_acc[:, c * width : (c + 1) * width].T.astype(BF16)
        turned = turned.reshape(per_chan, xs, share, width)
        for x in range(xs):
            p_send[x, c * per_chan : (c + 1) * per_chan] = turned[:, x]
    for x_off in range(1, xs):
        x = lax.rem(my_x + x_off, xs)
        send(
            p_send.at[x], p_xrecv.at[my_x], px_sems.at[0], px_sems.at[1], (my_yz * xs + x, mc)
        ).start()
    p_xrecv[my_x] = p_send[my_x]

    def back(turn):
        drain(recv2.at[pl.ds(0, seq_size - 1), turn], s2_recv.at[turn])
        stage(recv2[:, turn])
        r_acc[...] = jnp.zeros_like(r_acc)
        span = per_round * seq_size

        def go(at, carry):
            grad = jnp.concatenate(
                [
                    every(off * lb + at, seq_size, rows)
                    * diag_turned[
                        turn * per_round + off,
                        pl.ds(pl.multiple_of(at * seq_size, seq_size), seq_size),
                    ].astype(F32)
                    for off in range(per_round)
                ],
                axis=0,
            ).astype(BF16)
            out[at, turn * span : (turn + 1) * span] = grad
            made = matmul_nt(grad, vals[at])
            for c in range(chans):
                r_acc[c] += made[:, c * col : (c + 1) * col]
            return carry

        lax.fori_loop(0, lb, go, 0)
        for c in range(chans):
            for x in range(xs):
                r_send[turn, c * xs + x] = jnp.concatenate(
                    [
                        r_acc[c, pl.ds(off * seq_size + x, yzs, stride=xs), :]
                        for off in range(per_round)
                    ],
                    axis=0,
                ).astype(BF16)
        over_group(r_send.at[turn], r_recv.at[turn], rg_send.at[turn], rg_recv.at[turn])

    def right_rows(turn):
        summed = group_sum(r_recv.at[turn], rg_recv.at[turn])
        for off in range(per_round):
            r_rows[pl.ds(turn * per_round + off, yzs, stride=lb), :] = summed[
                off * yzs : (off + 1) * yzs
            ]

    back(0)
    back(1)
    middle = block // 2

    def early_part(at, carry):
        out_acc[at] = matmul(frt[:, :middle], out[at, :middle])
        return carry

    lax.fori_loop(0, lb, early_part, 0)
    back(2)
    back(3)

    def late_part(at, carry):
        total = out_acc[at] + matmul(frt[:, middle:], out[at, middle:])
        out[at] = (total * gate[at].astype(F32)).astype(BF16)
        pltpu.make_async_copy(out.at[at], input_grad_hbm.at[at], out_sem).start()
        return carry

    lax.fori_loop(0, lb, late_part, 0)
    over_yz(group_sum(l_recv, lg_recv).reshape(l_ysend.shape), l_ysend, l_yrecv, ly_sems)
    drain(p_xrecv.at[pl.ds(0, xs - 1)], px_sems.at[1])
    over_yz(jnp.sum(p_xrecv[...].astype(F32), axis=0), p_ysend, p_yrecv, py_sems)
    for turn in range(ROUNDS):
        right_rows(turn)
    over_yz(r_rows[...].reshape(r_ysend.shape), r_ysend, r_yrecv, ry_sems)

    for turn in range(ROUNDS):
        part = pl.ds(turn * per_round, per_round)
        drain(cot.at[mc, part], far_send.at[turn])
        drain(cot.at[mc, part], sib_send.at[turn])
        drain(cot.at[far, part], fwd_send.at[turn])
        drain(send2.at[turn, pl.ds(0, seq_size - 1)], s2_send.at[turn])
        drain(r_send.at[turn, pl.ds(0, xs * chans - 1)], rg_send.at[turn])
    drain(send1.at[pl.ds(0, seq_size - 1)], s1_send)
    drain(l_send.at[pl.ds(0, xs * chans - 1)], lg_send)
    drain(p_send.at[pl.ds(0, xs - 1)], px_sems.at[0])
    for sends, sems in ((p_ysend, py_sems), (l_ysend, ly_sems), (r_ysend, ry_sems)):
        drain(sends.at[pl.ds(0, yzs - 1)], sems.at[0])
    drain(out, out_sem)
    stores = [
        pltpu.make_async_copy(proj_grad, proj_grad_hbm, small_sem.at[0]),
        pltpu.make_async_copy(left_grad, left_grad_hbm, small_sem.at[1]),
        pltpu.make_async_copy(right_grad, right_grad_hbm, small_sem.at[2]),
    ]
    left_grad[...] = yz_sum(l_yrecv, ly_sems) * scale
    stores[1].start()
    proj_grad[...] = yz_sum(p_yrecv, py_sems) * (1.0 / block)
    stores[0].start()
    right_grad[...] = yz_sum(r_yrecv, ry_sems) * scale
    stores[2].start()
    for store in stores:
        store.wait()


def copy_kernel(*refs):
    srcs, dsts, held, sems = refs[:4], refs[4:8], refs[8:12], refs[12]
    lb = srcs[0].shape[0]
    hops = [(srcs[0].at[at], held[0].at[at], dsts[0].at[at]) for at in range(lb)]
    hops += list(zip(srcs[1:], held[1:], dsts[1:]))
    loads = [pltpu.make_async_copy(a, b, sems.at[0, n]) for n, (a, b, c) in enumerate(hops)]
    stores = [pltpu.make_async_copy(b, c, sems.at[1, n]) for n, (a, b, c) in enumerate(hops)]
    for load in loads:
        load.start()
    for load, store in zip(loads, stores):
        load.wait()
        store.start()
    for store in stores:
        store.wait()


def on_device(activation, gating, kernel_diag, cotangent, factor_right, factor_left, projection):
    row_count, width = activation.shape
    block = factor_right.shape[0]
    lb = row_count // block
    full = projection.shape[1]
    seq_size = lax.axis_size("seq")
    chans = lax.axis_size("chan")
    cube = (lb, block, width)
    share = full // seq_size
    col = block // chans
    xs = min(4, seq_size // 2)
    yzs = seq_size // xs
    dma = pltpu.SemaphoreType.DMA
    per_round = lb // ROUNDS
    span = per_round * seq_size

    def small(*lead):
        return pltpu.VMEM(lead + (lb, col), F32)

    scratch = [
        pltpu.VMEM(cube, BF16),
        pltpu.VMEM(cube, BF16),
        pltpu.VMEM(cube, BF16),
        pltpu.VMEM((chans,) + cube, BF16),
        pltpu.VMEM((block, block), BF16),
        pltpu.VMEM((block, block), BF16),
        pltpu.VMEM((width, full), BF16),
        pltpu.VMEM((block, block), BF16),
        pltpu.VMEM((block, block), BF16),
        pltpu.VMEM(cube, BF16),
        pltpu.VMEM(cube, BF16),
        pltpu.VMEM((seq_size, lb * lb, width), BF16),
        pltpu.VMEM((seq_size, lb * lb, width), BF16),
        pltpu.VMEM(cube, BF16),
        pltpu.VMEM((ROUNDS, seq_size, per_round * lb, width), BF16),
        pltpu.VMEM((seq_size, ROUNDS, per_round * lb, width), BF16),
        pltpu.VMEM((width // LANES, block * lb, LANES), F32),
        pltpu.VMEM(cube, BF16),
        pltpu.VMEM(cube, F32),
        pltpu.VMEM((width, full), F32),
        pltpu.VMEM((xs, yzs, share, width), BF16),
        pltpu.VMEM((xs, yzs, share, width), BF16),
        pltpu.VMEM((yzs, share, width), BF16),
        pltpu.VMEM((yzs, share, width), BF16),
        pltpu.VMEM((block, block), F32),
        pltpu.VMEM((chans * xs, yzs * lb, col), BF16),
        pltpu.VMEM((chans * xs, yzs * lb, col), BF16),
        small(yzs), small(yzs),
        pltpu.VMEM((chans, span, col), F32),
        pltpu.VMEM((ROUNDS, chans * xs, span // xs, col), BF16),
        pltpu.VMEM((ROUNDS, chans * xs, span // xs, col), BF16),
        pltpu.VMEM((yzs * lb, col), F32),
        small(yzs), small(yzs),
        pltpu.VMEM((share, width), F32), small(), small(),
        dma((7,)), dma, dma((3,)),
    ] + [dma((ROUNDS,))] * 6 + [
        dma, dma, dma((ROUNDS,)), dma((ROUNDS,)), dma((ROUNDS,)), dma((ROUNDS,)), dma, dma,
    ] + [dma((2,))] * 4
    any_space = pl.BlockSpec(memory_space=pl.ANY)
    shapes = [
        jax.ShapeDtypeStruct(cube, BF16),
        jax.ShapeDtypeStruct((share, width), F32),
        jax.ShapeDtypeStruct((lb, col), F32),
        jax.ShapeDtypeStruct((lb, col), F32),
    ]
    results = pl.pallas_call(
        functools.partial(kernel, float((block * full) ** (-0.5))),
        out_shape=shapes,
        in_specs=[any_space] * 7,
        out_specs=[any_space] * 4,
        scratch_shapes=scratch,
        compiler_params=pltpu.CompilerParams(
            collective_id=0, has_side_effects=True, vmem_limit_bytes=58 * 1024 * 1024
        ),
        cost_estimate=pl.CostEstimate(
            flops=20 * row_count * block * width, bytes_accessed=12 * row_count * width,
            transcendentals=0,
        ),
        name="monarch_backward",
    )(
        activation.reshape(cube), gating.reshape(cube), kernel_diag.reshape(cube),
        cotangent.reshape(cube), factor_right, factor_left, projection,
    )
    input_grad, proj_grad, right_grad, left_grad = pl.pallas_call(
        copy_kernel,
        out_shape=shapes,
        in_specs=[any_space] * 4,
        out_specs=[any_space] * 4,
        scratch_shapes=[pltpu.VMEM(shape.shape, shape.dtype) for shape in shapes]
        + [dma((2, lb + 3))],
        name="copy_results",
    )(*results)
    return (input_grad.reshape(row_count, width), proj_grad.T, right_grad, left_grad)


def solution(mesh):
    in_specs = (
        P("seq", "chan"),
        P("seq", "chan"),
        P("seq", "chan"),
        P("seq", "chan"),
        P(),
        P(),
        P("chan", None),
    )
    out_specs = (P("seq", "chan"), P("chan", "seq"), P("seq", "chan"), P("seq", "chan"))
    return jax.shard_map(
        on_device, mesh=mesh, in_specs=in_specs, out_specs=out_specs, check_vma=False
    )
```

```python
import functools

import jax
import jax.numpy as jnp
from jax import lax
from jax.experimental import pallas as pl
from jax.experimental.pallas import tpu as pltpu
from jax.sharding import PartitionSpec as P

ROUNDS = 4
LANES = 128
FIRST_CROSS = 1
SECOND_CROSS = 3
F32 = jnp.float32
BF16 = jnp.bfloat16


def matmul(left, right):
    return jnp.dot(left, right, preferred_element_type=F32)


def matmul_nt(left, right):
    return lax.dot_general(left, right, (((1,), (1,)), ((), ())), preferred_element_type=F32)


def kernel(
    scale,
    act_hbm, gate_hbm, diag_hbm, cot_hbm, right_hbm, left_hbm, proj_hbm,
    input_grad_hbm, proj_grad_hbm, right_grad_hbm, left_grad_hbm,
    act, gate, diag, cot, fr, fl, proj, frt, flt, diag_turned,
    vals, send1, recv1, mg, send2, recv2, staging, out, out_acc,
    p_acc, p_send, p_xrecv, p_ysend, p_yrecv,
    l_acc, l_send, l_recv, l_ysend, l_yrecv,
    r_acc, r_send, r_recv, r_rows, r_ysend, r_yrecv,
    proj_grad, right_grad, left_grad,
    in_sem, out_sem, small_sem,
    far_send, far_recv, sib_send, sib_recv, fwd_send, fwd_recv,
    s1_send, s1_recv, s2_send, s2_recv, rg_send, rg_recv, lg_send, lg_recv,
    px_sems, py_sems, ly_sems, ry_sems,
):
    seq_size = recv1.shape[0]
    lb, block, width = vals.shape
    per_round = lb // ROUNDS
    rows = per_round * lb
    chans = cot.shape[0]
    me = lax.axis_index("seq")
    mc = lax.axis_index("chan")
    sibling = mc + 1 - 2 * lax.rem(mc, 2)
    far = lax.rem(mc + 2, 4)
    far_sibling = 3 - mc
    my_lo = mc // 2
    my_core = lax.rem(mc, 2)
    half = seq_size // 2
    xs = p_send.shape[0]
    zs = half // xs
    yzs = seq_size // xs
    my_half = me // half
    my_z = lax.rem(me, half) // xs
    my_x = lax.rem(me, xs)
    my_yz = me // xs

    barrier = pltpu.get_barrier_semaphore()

    def greet(step, carry):
        other = lax.rem(me + step, seq_size)
        pl.semaphore_signal(
            barrier, inc=1, device_id=(other, mc), device_id_type=pl.DeviceIdType.MESH
        )
        return carry

    group = [
        (lax.rem(my_x + x_off, xs), chan)
        for x_off in range(xs)
        for chan in (mc, sibling)
        if x_off > 0 or chan is not mc
    ]
    for x, chan in group:
        if chan is not mc:
            pl.semaphore_signal(
                barrier, inc=1, device_id=(my_yz * xs + x, chan),
                device_id_type=pl.DeviceIdType.MESH,
            )

    def greet_far(step, carry):
        other = lax.rem(my_yz + step, yzs) * xs + my_x
        pl.semaphore_signal(
            barrier, inc=1, device_id=(other, far), device_id_type=pl.DeviceIdType.MESH
        )
        return carry

    lax.fori_loop(0, yzs, greet_far, 0)
    lax.fori_loop(1, seq_size, greet, 0)

    loads = [
        pltpu.make_async_copy(src, dst, in_sem.at[at])
        for at, (src, dst) in enumerate(
            (
                (act_hbm, act),
                (gate_hbm, gate),
                (right_hbm, fr),
                (diag_hbm, diag),
                (cot_hbm, cot.at[mc]),
                (proj_hbm, proj),
                (left_hbm, fl),
            )
        )
    ]
    for load in loads:
        load.start()

    def send(src, dst, send_sem, recv_sem, device):
        return pltpu.make_async_remote_copy(
            src_ref=src, dst_ref=dst, send_sem=send_sem, recv_sem=recv_sem,
            device_id=device, device_id_type=pl.DeviceIdType.MESH,
        )

    def drain(ref, sem):
        pltpu.make_async_copy(ref, ref, sem).wait()

    def place(step, cross):
        turn = lax.rem(step, zs)
        z_off = (2 * lax.rem(turn, 2) - 1) * ((turn + 1) // 2)
        x_off = step // zs
        z = lax.rem(my_z + z_off + zs, zs)
        x = lax.rem(my_x + x_off, xs)
        return lax.rem(my_half + cross, 2) * half + z * xs + x

    def first_sends(cross, first, count):
        part = pl.ds(first * lb, count * lb)

        def go(step, carry):
            other = place(step, cross)
            send(
                send1.at[other, part], recv1.at[me, part], s1_send, s1_recv, (other, mc)
            ).start()
            return carry

        lax.fori_loop(1 - cross, half, go, 0)

    def second_sends(turn, cross):
        def go(step, carry):
            other = place(step, cross)
            send(
                send2.at[turn, other], recv2.at[me, turn], s2_send.at[turn], s2_recv.at[turn],
                (other, mc),
            ).start()
            return carry

        lax.fori_loop(1 - cross, half, go, 0)

    for load in loads[:4]:
        load.wait()

    for pair in range(lb // 2):
        pieces = []
        for at in (2 * pair, 2 * pair + 1):
            value = (act[at].astype(F32) * gate[at].astype(F32)).astype(BF16)
            vals[at] = value
            made = matmul(fr[...], value) * diag[at].astype(F32)
            pieces.append(made.reshape(seq_size, lb, width))
        send1[:, 2 * pair * lb : (2 * pair + 2) * lb, :] = jnp.concatenate(
            pieces, axis=1
        ).astype(BF16)
        if pair == 0:
            pl.semaphore_wait(barrier, seq_size - 1 + xs + yzs)
            for turn in range(ROUNDS):
                part = pl.ds(turn * per_round, per_round)
                send(
                    cot_hbm.at[part], cot.at[mc, part], far_send.at[turn], far_recv.at[turn], (me, far)
                ).start()
            for turn in range(ROUNDS):
                part = pl.ds(turn * per_round, per_round)
                send(
                    cot_hbm.at[part], cot.at[mc, part], sib_send.at[turn], sib_recv.at[turn],
                    (me, sibling),
                ).start()
        first_sends(0, 2 * pair, 2)
    recv1[me] = send1[me]

    for load in loads[4:]:
        load.wait()
    flt[...] = fl[...].T

    def stage(blocks):
        count = blocks.shape[0] * blocks.shape[1]
        flat = blocks.reshape(count, width).astype(F32)
        for part in range(width // LANES):
            staging[part, :count] = flat[:, part * LANES : (part + 1) * LANES]

    def every(start, count, stride):
        return jnp.concatenate(
            [
                staging[part, pl.ds(start, count, stride=stride), :]
                for part in range(width // LANES)
            ],
            axis=1,
        )

    for col in range(block // LANES):
        staging[0, col * block : (col + 1) * block] = fr[
            :, col * LANES : (col + 1) * LANES
        ].astype(F32)
    for kk in range(lb):
        turned = jnp.concatenate(
            [
                staging[0, pl.ds(col * block + kk, seq_size, stride=lb), :]
                for col in range(block // LANES)
            ],
            axis=1,
        )
        frt[:, kk * seq_size : (kk + 1) * seq_size] = turned.T.astype(BF16)
    stage(diag[...])

    def turn_diag(kk, carry):
        diag_turned[kk] = every(kk, block, lb).astype(BF16)
        return carry

    lax.fori_loop(0, lb, turn_diag, 0)

    for turn in range(ROUNDS):
        part = pl.ds(turn * per_round, per_round)
        drain(cot.at[far, part], far_recv.at[turn])
        forward = send(
            cot.at[far, part], cot.at[far, part], fwd_send.at[turn], fwd_recv.at[turn],
            (me, sibling),
        )
        forward.start()
        drain(cot.at[sibling, part], sib_recv.at[turn])
        drain(cot.at[far_sibling, part], fwd_recv.at[turn])
        pieces = []
        for off in range(per_round):
            at = turn * per_round + off
            total = matmul_nt(cot[0, at], proj[:, :width])
            for c in range(1, chans):
                total += matmul_nt(cot[c, at], proj[:, c * width : (c + 1) * width])
            up = total.astype(BF16)
            mg[at] = up
            pieces.append(matmul(flt[...], up).reshape(seq_size, lb, width))
        send2[turn] = jnp.concatenate(pieces, axis=1).astype(BF16)
        second_sends(turn, 0)
        recv2[me, turn] = send2[turn, me]
        if turn == FIRST_CROSS:
            first_sends(1, 0, lb)
        if turn == SECOND_CROSS:
            for earlier in range(turn):
                second_sends(earlier, 1)
        if turn >= SECOND_CROSS:
            second_sends(turn, 1)

    drain(recv1.at[pl.ds(0, seq_size - 1)], s1_recv)
    stage(recv1[...])
    p_acc[...] = jnp.zeros_like(p_acc)
    l_acc[...] = jnp.zeros_like(l_acc)

    def mixed_part(pair, carry):
        at = pair * 2
        got = jnp.concatenate([every(at, block, lb), every(at + 1, block, lb)], axis=1)
        got = got.astype(BF16)
        l_acc[...] += matmul_nt(jnp.concatenate([mg[at], mg[at + 1]], axis=1), got)
        mixed = matmul(fl[...], got).astype(BF16)
        turned = jnp.concatenate([mixed[:, :width].T, mixed[:, width:].T], axis=1)
        for c in range(chans):
            p_acc[:, c * width : (c + 1) * width] += matmul(
                turned, cot[c, pl.ds(at, 2)].reshape(2 * block, width)
            )
        return carry

    lax.fori_loop(0, lb // 2, mixed_part, 0)

    def over_group(sends, recvs, ssem, rsem):
        mine = my_core * xs + my_x
        for x, chan in group:
            send(
                sends.at[lax.rem(chan, 2) * xs + x], recvs.at[mine], ssem, rsem,
                (my_yz * xs + x, chan),
            ).start()
        recvs[mine] = sends[mine]

    def group_sum(recvs, rsem):
        drain(recvs.at[pl.ds(0, 2 * xs - 1)], rsem)
        return jnp.sum(recvs[...].astype(F32), axis=0)

    def over_yz(total, sends, recvs, sems, pair):
        sends[...] = total.astype(sends.dtype)
        near = my_lo * yzs if pair else 0

        def go(first, chan):
            def step_to(step, carry):
                other = lax.rem(my_yz + step, yzs)
                send(
                    sends.at[first + other], recvs.at[near + my_yz], sems.at[0], sems.at[1],
                    (other * xs + my_x, chan),
                ).start()
                return carry

            return step_to

        if pair:
            lax.fori_loop(0, yzs, go((1 - my_lo) * yzs, far), 0)
        lax.fori_loop(1, yzs, go(near, mc), 0)
        recvs[near + my_yz] = sends[near + my_yz]

    def yz_sum(recvs, sems):
        drain(recvs.at[pl.ds(0, recvs.shape[0] - 1)], sems.at[1])
        return jnp.sum(recvs[...].astype(F32), axis=0)

    col = block // chans
    split = l_acc[...].reshape(yzs, xs, lb, block)
    for c in range(chans):
        for x in range(xs):
            l_send[c % 2 * xs + x, c // 2] = (
                split[:, x, :, c * col : (c + 1) * col].reshape(yzs * lb, col).astype(BF16)
            )
    over_group(l_send, l_recv, lg_send, lg_recv)
    share = p_send.shape[2]
    per_chan = yzs // chans
    for c in range(chans):
        turned = p_acc[:, c * width : (c + 1) * width].T.astype(BF16)
        turned = turned.reshape(per_chan, xs, share, width)
        for x in range(xs):
            p_send[x, c * per_chan : (c + 1) * per_chan] = turned[:, x]
    for x_off in range(1, xs):
        x = lax.rem(my_x + x_off, xs)
        send(
            p_send.at[x], p_xrecv.at[my_x], px_sems.at[0], px_sems.at[1], (my_yz * xs + x, mc)
        ).start()
    p_xrecv[my_x] = p_send[my_x]

    def back(turn):
        drain(recv2.at[pl.ds(0, seq_size - 1), turn], s2_recv.at[turn])
        stage(recv2[:, turn])
        r_acc[...] = jnp.zeros_like(r_acc)
        span = per_round * seq_size

        def grad_of(at):
            return jnp.concatenate(
                [
                    every(off * lb + at, seq_size, rows)
                    * diag_turned[
                        turn * per_round + off,
                        pl.ds(pl.multiple_of(at * seq_size, seq_size), seq_size),
                    ].astype(F32)
                    for off in range(per_round)
                ],
                axis=0,
            ).astype(BF16)

        def go(pair, carry):
            at = pair * 2
            grads = [grad_of(at), grad_of(at + 1)]
            out[at, turn * span : (turn + 1) * span] = grads[0]
            out[at + 1, turn * span : (turn + 1) * span] = grads[1]
            made = matmul_nt(
                jnp.concatenate(grads, axis=1),
                jnp.concatenate([vals[at], vals[at + 1]], axis=1),
            )
            for c in range(chans):
                r_acc[c] += made[:, c * col : (c + 1) * col]
            return carry

        lax.fori_loop(0, lb // 2, go, 0)
        for c in range(chans):
            for x in range(xs):
                r_send[turn, c % 2 * xs + x, c // 2] = jnp.concatenate(
                    [
                        r_acc[c, pl.ds(off * seq_size + x, yzs, stride=xs), :]
                        for off in range(per_round)
                    ],
                    axis=0,
                ).astype(BF16)
        over_group(r_send.at[turn], r_recv.at[turn], rg_send.at[turn], rg_recv.at[turn])

    def right_rows(turn):
        summed = group_sum(r_recv.at[turn], rg_recv.at[turn])
        for chip in range(2):
            for off in range(per_round):
                r_rows[chip, pl.ds(turn * per_round + off, yzs, stride=lb), :] = summed[
                    chip, off * yzs : (off + 1) * yzs
                ]

    back(0)
    back(1)
    middle = block // 2

    def early_part(at, carry):
        out_acc[at] = matmul(frt[:, :middle], out[at, :middle])
        return carry

    lax.fori_loop(0, lb, early_part, 0)
    back(2)
    over_yz(group_sum(l_recv, lg_recv).reshape(l_ysend.shape), l_ysend, l_yrecv, ly_sems, True)
    drain(p_xrecv.at[pl.ds(0, xs - 1)], px_sems.at[1])
    over_yz(jnp.sum(p_xrecv[...].astype(F32), axis=0), p_ysend, p_yrecv, py_sems, False)
    back(3)

    def late_part(at, carry):
        total = out_acc[at] + matmul(frt[:, middle:], out[at, middle:])
        out[at] = (total * gate[at].astype(F32)).astype(BF16)
        pltpu.make_async_copy(out.at[at], input_grad_hbm.at[at], out_sem).start()
        return carry

    lax.fori_loop(0, lb, late_part, 0)
    for turn in range(ROUNDS):
        right_rows(turn)
    over_yz(r_rows[...].reshape(r_ysend.shape), r_ysend, r_yrecv, ry_sems, True)

    for turn in range(ROUNDS):
        part = pl.ds(turn * per_round, per_round)
        drain(cot.at[mc, part], far_send.at[turn])
        drain(cot.at[mc, part], sib_send.at[turn])
        drain(cot.at[far, part], fwd_send.at[turn])
        drain(send2.at[turn, pl.ds(0, seq_size - 1)], s2_send.at[turn])
        drain(r_send.at[turn, pl.ds(0, 2 * xs - 1)], rg_send.at[turn])
    drain(send1.at[pl.ds(0, seq_size - 1)], s1_send)
    drain(l_send.at[pl.ds(0, 2 * xs - 1)], lg_send)
    drain(p_send.at[pl.ds(0, xs - 1)], px_sems.at[0])
    for sends, sems in ((p_ysend, py_sems), (l_ysend, ly_sems), (r_ysend, ry_sems)):
        drain(sends.at[pl.ds(0, sends.shape[0] - 1)], sems.at[0])
    drain(out, out_sem)
    stores = [
        pltpu.make_async_copy(proj_grad, proj_grad_hbm, small_sem.at[0]),
        pltpu.make_async_copy(left_grad, left_grad_hbm, small_sem.at[1]),
        pltpu.make_async_copy(right_grad, right_grad_hbm, small_sem.at[2]),
    ]
    left_grad[...] = yz_sum(l_yrecv, ly_sems) * scale
    stores[1].start()
    proj_grad[...] = yz_sum(p_yrecv, py_sems) * (1.0 / block)
    stores[0].start()
    right_grad[...] = yz_sum(r_yrecv, ry_sems) * scale
    stores[2].start()
    for store in stores:
        store.wait()


def copy_kernel(*refs):
    srcs, dsts, held, sems = refs[:4], refs[4:8], refs[8:12], refs[12]
    lb = srcs[0].shape[0]
    hops = [(srcs[0].at[at], held[0].at[at], dsts[0].at[at]) for at in range(lb)]
    hops += list(zip(srcs[1:], held[1:], dsts[1:]))
    loads = [pltpu.make_async_copy(a, b, sems.at[0, n]) for n, (a, b, c) in enumerate(hops)]
    stores = [pltpu.make_async_copy(b, c, sems.at[1, n]) for n, (a, b, c) in enumerate(hops)]
    for load in loads:
        load.start()
    for load, store in zip(loads, stores):
        load.wait()
        store.start()
    for store in stores:
        store.wait()


def on_device(activation, gating, kernel_diag, cotangent, factor_right, factor_left, projection):
    row_count, width = activation.shape
    block = factor_right.shape[0]
    lb = row_count // block
    full = projection.shape[1]
    seq_size = lax.axis_size("seq")
    chans = lax.axis_size("chan")
    cube = (lb, block, width)
    share = full // seq_size
    col = block // chans
    xs = min(4, seq_size // 2)
    yzs = seq_size // xs
    dma = pltpu.SemaphoreType.DMA
    per_round = lb // ROUNDS
    span = per_round * seq_size

    def small(*lead):
        return pltpu.VMEM(lead + (lb, col), F32)

    scratch = [
        pltpu.VMEM(cube, BF16),
        pltpu.VMEM(cube, BF16),
        pltpu.VMEM(cube, BF16),
        pltpu.VMEM((chans,) + cube, BF16),
        pltpu.VMEM((block, block), BF16),
        pltpu.VMEM((block, block), BF16),
        pltpu.VMEM((width, full), BF16),
        pltpu.VMEM((block, block), BF16),
        pltpu.VMEM((block, block), BF16),
        pltpu.VMEM(cube, BF16),
        pltpu.VMEM(cube, BF16),
        pltpu.VMEM((seq_size, lb * lb, width), BF16),
        pltpu.VMEM((seq_size, lb * lb, width), BF16),
        pltpu.VMEM(cube, BF16),
        pltpu.VMEM((ROUNDS, seq_size, per_round * lb, width), BF16),
        pltpu.VMEM((seq_size, ROUNDS, per_round * lb, width), BF16),
        pltpu.VMEM((width // LANES, block * lb, LANES), F32),
        pltpu.VMEM(cube, BF16),
        pltpu.VMEM(cube, F32),
        pltpu.VMEM((width, full), F32),
        pltpu.VMEM((xs, yzs, share, width), BF16),
        pltpu.VMEM((xs, yzs, share, width), BF16),
        pltpu.VMEM((yzs, share, width), BF16),
        pltpu.VMEM((yzs, share, width), BF16),
        pltpu.VMEM((block, block), F32),
        pltpu.VMEM((2 * xs, 2, yzs * lb, col), BF16),
        pltpu.VMEM((2 * xs, 2, yzs * lb, col), BF16),
        small(2 * yzs), small(2 * yzs),
        pltpu.VMEM((chans, span, col), F32),
        pltpu.VMEM((ROUNDS, 2 * xs, 2, span // xs, col), BF16),
        pltpu.VMEM((ROUNDS, 2 * xs, 2, span // xs, col), BF16),
        pltpu.VMEM((2, yzs * lb, col), F32),
        small(2 * yzs), small(2 * yzs),
        pltpu.VMEM((share, width), F32), small(), small(),
        dma((7,)), dma, dma((3,)),
    ] + [dma((ROUNDS,))] * 6 + [
        dma, dma, dma((ROUNDS,)), dma((ROUNDS,)), dma((ROUNDS,)), dma((ROUNDS,)), dma, dma,
    ] + [dma((2,))] * 4
    any_space = pl.BlockSpec(memory_space=pl.ANY)
    shapes = [
        jax.ShapeDtypeStruct(cube, BF16),
        jax.ShapeDtypeStruct((share, width), F32),
        jax.ShapeDtypeStruct((lb, col), F32),
        jax.ShapeDtypeStruct((lb, col), F32),
    ]
    results = pl.pallas_call(
        functools.partial(kernel, float((block * full) ** (-0.5))),
        out_shape=shapes,
        in_specs=[any_space] * 7,
        out_specs=[any_space] * 4,
        scratch_shapes=scratch,
        compiler_params=pltpu.CompilerParams(
            collective_id=0, has_side_effects=True, vmem_limit_bytes=58 * 1024 * 1024
        ),
        cost_estimate=pl.CostEstimate(
            flops=20 * row_count * block * width, bytes_accessed=12 * row_count * width,
            transcendentals=0,
        ),
        name="monarch_backward",
    )(
        activation.reshape(cube), gating.reshape(cube), kernel_diag.reshape(cube),
        cotangent.reshape(cube), factor_right, factor_left, projection,
    )
    input_grad, proj_grad, right_grad, left_grad = pl.pallas_call(
        copy_kernel,
        out_shape=shapes,
        in_specs=[any_space] * 4,
        out_specs=[any_space] * 4,
        scratch_shapes=[pltpu.VMEM(shape.shape, shape.dtype) for shape in shapes]
        + [dma((2, lb + 3))],
        name="copy_results",
    )(*results)
    return (input_grad.reshape(row_count, width), proj_grad.T, right_grad, left_grad)


def solution(mesh):
    in_specs = (
        P("seq", "chan"),
        P("seq", "chan"),
        P("seq", "chan"),
        P("seq", "chan"),
        P(),
        P(),
        P("chan", None),
    )
    out_specs = (P("seq", "chan"), P("chan", "seq"), P("seq", "chan"), P("seq", "chan"))
    return jax.shard_map(
        on_device, mesh=mesh, in_specs=in_specs, out_specs=out_specs, check_vma=False
    )
```

```python
import functools

import jax
import jax.numpy as jnp
from jax import lax
from jax.experimental import pallas as pl
from jax.experimental.pallas import tpu as pltpu
from jax.sharding import PartitionSpec as P

ROUNDS = 4
LANES = 128
FIRST_CROSS = 1
SECOND_CROSS = 3
F32 = jnp.float32
BF16 = jnp.bfloat16


def matmul(left, right):
    return jnp.dot(left, right, preferred_element_type=F32)


def matmul_nt(left, right):
    return lax.dot_general(left, right, (((1,), (1,)), ((), ())), preferred_element_type=F32)


def kernel(
    scale,
    act_hbm, gate_hbm, diag_hbm, cot_hbm, right_hbm, left_hbm, proj_hbm,
    input_grad_hbm, proj_grad_hbm, right_grad_hbm, left_grad_hbm,
    act, gate, diag, cot, fr, fl, proj, frt, flt, diag_turned,
    vals, send1, recv1, mg, send2, recv2, staging, out, out_acc,
    p_acc, p_send, p_xrecv, p_ysend, p_yrecv,
    l_acc, l_send, l_recv, l_ysend, l_yrecv,
    r_acc, r_send, r_recv, r_rows, r_ysend, r_yrecv,
    proj_grad, right_grad, left_grad,
    in_sem, out_sem, small_sem,
    far_send, far_recv, sib_send, sib_recv, fwd_send, fwd_recv,
    s1_send, s1_recv, s2_send, s2_recv, rg_send, rg_recv, lg_send, lg_recv,
    px_sems, py_sems, ly_sems, ry_sems,
):
    seq_size = recv1.shape[0]
    lb, block, width = vals.shape
    per_round = lb // ROUNDS
    rows = per_round * lb
    chans = cot.shape[0]
    me = lax.axis_index("seq")
    mc = lax.axis_index("chan")
    sibling = mc + 1 - 2 * lax.rem(mc, 2)
    far = lax.rem(mc + 2, 4)
    far_sibling = 3 - mc
    my_lo = mc // 2
    my_core = lax.rem(mc, 2)
    half = seq_size // 2
    xs = p_send.shape[0]
    zs = half // xs
    yzs = seq_size // xs
    my_half = me // half
    my_z = lax.rem(me, half) // xs
    my_x = lax.rem(me, xs)
    my_yz = me // xs

    barrier = pltpu.get_barrier_semaphore()

    def greet(step, carry):
        other = lax.rem(me + step, seq_size)
        pl.semaphore_signal(
            barrier, inc=1, device_id=(other, mc), device_id_type=pl.DeviceIdType.MESH
        )
        return carry

    group = [
        (lax.rem(my_x + x_off, xs), chan)
        for x_off in range(xs)
        for chan in (mc, sibling)
        if x_off > 0 or chan is not mc
    ]
    for x, chan in group:
        if chan is not mc:
            pl.semaphore_signal(
                barrier, inc=1, device_id=(my_yz * xs + x, chan),
                device_id_type=pl.DeviceIdType.MESH,
            )

    def greet_far(step, carry):
        other = lax.rem(my_yz + step, yzs) * xs + my_x
        pl.semaphore_signal(
            barrier, inc=1, device_id=(other, far), device_id_type=pl.DeviceIdType.MESH
        )
        return carry

    lax.fori_loop(0, yzs, greet_far, 0)
    lax.fori_loop(1, seq_size, greet, 0)

    loads = [
        pltpu.make_async_copy(src, dst, in_sem.at[at])
        for at, (src, dst) in enumerate(
            (
                (act_hbm, act),
                (gate_hbm, gate),
                (right_hbm, fr),
                (diag_hbm, diag),
                (cot_hbm, cot.at[mc]),
                (proj_hbm, proj),
                (left_hbm, fl),
            )
        )
    ]
    for load in loads:
        load.start()

    def send(src, dst, send_sem, recv_sem, device):
        return pltpu.make_async_remote_copy(
            src_ref=src, dst_ref=dst, send_sem=send_sem, recv_sem=recv_sem,
            device_id=device, device_id_type=pl.DeviceIdType.MESH,
        )

    def drain(ref, sem):
        pltpu.make_async_copy(ref, ref, sem).wait()

    def place(step, cross):
        turn = lax.rem(step, zs)
        z_off = (2 * lax.rem(turn, 2) - 1) * ((turn + 1) // 2)
        x_off = step // zs
        z = lax.rem(my_z + z_off + zs, zs)
        x = lax.rem(my_x + x_off, xs)
        return lax.rem(my_half + cross, 2) * half + z * xs + x

    def first_sends(cross, first, count):
        part = pl.ds(first * lb, count * lb)

        def go(step, carry):
            other = place(step, cross)
            send(
                send1.at[other, part], recv1.at[me, part], s1_send, s1_recv, (other, mc)
            ).start()
            return carry

        lax.fori_loop(1 - cross, half, go, 0)

    def second_sends(turn, cross):
        def go(step, carry):
            other = place(step, cross)
            send(
                send2.at[turn, other], recv2.at[me, turn], s2_send.at[turn], s2_recv.at[turn],
                (other, mc),
            ).start()
            return carry

        lax.fori_loop(1 - cross, half, go, 0)

    for load in loads[:4]:
        load.wait()

    for pair in range(lb // 2):
        pieces = []
        for at in (2 * pair, 2 * pair + 1):
            value = (act[at].astype(F32) * gate[at].astype(F32)).astype(BF16)
            vals[at] = value
            made = matmul(fr[...], value) * diag[at].astype(F32)
            pieces.append(made.reshape(seq_size, lb, width))
        send1[:, 2 * pair * lb : (2 * pair + 2) * lb, :] = jnp.concatenate(
            pieces, axis=1
        ).astype(BF16)
        if pair == 0:
            pl.semaphore_wait(barrier, seq_size - 1 + xs + yzs)
            for turn in range(ROUNDS):
                part = pl.ds(turn * per_round, per_round)
                send(
                    cot_hbm.at[part], cot.at[mc, part], far_send.at[turn], far_recv.at[turn], (me, far)
                ).start()
            for turn in range(ROUNDS):
                part = pl.ds(turn * per_round, per_round)
                send(
                    cot_hbm.at[part], cot.at[mc, part], sib_send.at[turn], sib_recv.at[turn],
                    (me, sibling),
                ).start()
        first_sends(0, 2 * pair, 2)
    recv1[me] = send1[me]

    for load in loads[4:]:
        load.wait()
    flt[...] = fl[...].T

    def stage(blocks):
        count = blocks.shape[0] * blocks.shape[1]
        flat = blocks.reshape(count, width).astype(F32)
        for part in range(width // LANES):
            staging[part, :count] = flat[:, part * LANES : (part + 1) * LANES]

    def every(start, count, stride):
        return jnp.concatenate(
            [
                staging[part, pl.ds(start, count, stride=stride), :]
                for part in range(width // LANES)
            ],
            axis=1,
        )

    for col in range(block // LANES):
        staging[0, col * block : (col + 1) * block] = fr[
            :, col * LANES : (col + 1) * LANES
        ].astype(F32)
    for kk in range(lb):
        turned = jnp.concatenate(
            [
                staging[0, pl.ds(col * block + kk, seq_size, stride=lb), :]
                for col in range(block // LANES)
            ],
            axis=1,
        )
        frt[:, kk * seq_size : (kk + 1) * seq_size] = turned.T.astype(BF16)
    stage(diag[...])

    def turn_diag(kk, carry):
        diag_turned[kk] = every(kk, block, lb).astype(BF16)
        return carry

    lax.fori_loop(0, lb, turn_diag, 0)

    for turn in range(ROUNDS):
        part = pl.ds(turn * per_round, per_round)
        drain(cot.at[far, part], far_recv.at[turn])
        forward = send(
            cot.at[far, part], cot.at[far, part], fwd_send.at[turn], fwd_recv.at[turn],
            (me, sibling),
        )
        forward.start()
        if turn == SECOND_CROSS:
            for earlier in range(turn):
                second_sends(earlier, 1)
        drain(cot.at[sibling, part], sib_recv.at[turn])
        drain(cot.at[far_sibling, part], fwd_recv.at[turn])
        pieces = []
        for off in range(per_round):
            at = turn * per_round + off
            total = matmul_nt(cot[0, at], proj[:, :width])
            for c in range(1, chans):
                total += matmul_nt(cot[c, at], proj[:, c * width : (c + 1) * width])
            up = total.astype(BF16)
            mg[at] = up
            pieces.append(matmul(flt[...], up).reshape(seq_size, lb, width))
        send2[turn] = jnp.concatenate(pieces, axis=1).astype(BF16)
        second_sends(turn, 0)
        recv2[me, turn] = send2[turn, me]
        if turn == FIRST_CROSS:
            first_sends(1, 0, lb)
        if turn >= SECOND_CROSS:
            second_sends(turn, 1)

    drain(recv1.at[pl.ds(0, seq_size - 1)], s1_recv)
    stage(recv1[...])
    p_acc[...] = jnp.zeros_like(p_acc)
    l_acc[...] = jnp.zeros_like(l_acc)

    def mixed_part(pair, carry):
        at = pair * 2
        got = jnp.concatenate([every(at, block, lb), every(at + 1, block, lb)], axis=1)
        got = got.astype(BF16)
        l_acc[...] += matmul_nt(jnp.concatenate([mg[at], mg[at + 1]], axis=1), got)
        mixed = matmul(fl[...], got).astype(BF16)
        turned = jnp.concatenate([mixed[:, :width].T, mixed[:, width:].T], axis=1)
        for c in range(chans):
            p_acc[:, c * width : (c + 1) * width] += matmul(
                turned, cot[c, pl.ds(at, 2)].reshape(2 * block, width)
            )
        return carry

    lax.fori_loop(0, lb // 2, mixed_part, 0)

    def over_group(sends, recvs, ssem, rsem):
        mine = my_core * xs + my_x
        for x, chan in group:
            send(
                sends.at[lax.rem(chan, 2) * xs + x], recvs.at[mine], ssem, rsem,
                (my_yz * xs + x, chan),
            ).start()
        recvs[mine] = sends[mine]

    def group_sum(recvs, rsem):
        drain(recvs.at[pl.ds(0, 2 * xs - 1)], rsem)
        return jnp.sum(recvs[...].astype(F32), axis=0)

    def over_yz(total, sends, recvs, sems, pair):
        sends[...] = total.astype(sends.dtype)
        near = my_lo * yzs if pair else 0

        def go(first, chan):
            def step_to(step, carry):
                other = lax.rem(my_yz + step, yzs)
                send(
                    sends.at[first + other], recvs.at[near + my_yz], sems.at[0], sems.at[1],
                    (other * xs + my_x, chan),
                ).start()
                return carry

            return step_to

        if pair:
            lax.fori_loop(0, yzs, go((1 - my_lo) * yzs, far), 0)
        lax.fori_loop(1, yzs, go(near, mc), 0)
        recvs[near + my_yz] = sends[near + my_yz]

    def yz_sum(recvs, sems):
        drain(recvs.at[pl.ds(0, recvs.shape[0] - 1)], sems.at[1])
        return jnp.sum(recvs[...].astype(F32), axis=0)

    col = block // chans
    split = l_acc[...].reshape(yzs, xs, lb, block)
    for c in range(chans):
        for x in range(xs):
            l_send[c % 2 * xs + x, c // 2] = (
                split[:, x, :, c * col : (c + 1) * col].reshape(yzs * lb, col).astype(BF16)
            )
    over_group(l_send, l_recv, lg_send, lg_recv)
    share = p_send.shape[2]
    per_chan = yzs // chans
    for c in range(chans):
        turned = p_acc[:, c * width : (c + 1) * width].T.astype(BF16)
        turned = turned.reshape(per_chan, xs, share, width)
        for x in range(xs):
            p_send[x, c * per_chan : (c + 1) * per_chan] = turned[:, x]
    for x_off in range(1, xs):
        x = lax.rem(my_x + x_off, xs)
        send(
            p_send.at[x], p_xrecv.at[my_x], px_sems.at[0], px_sems.at[1], (my_yz * xs + x, mc)
        ).start()
    p_xrecv[my_x] = p_send[my_x]

    def back(turn):
        drain(recv2.at[pl.ds(0, seq_size - 1), turn], s2_recv.at[turn])
        stage(recv2[:, turn])
        r_acc[...] = jnp.zeros_like(r_acc)
        span = per_round * seq_size

        def grad_of(at):
            return jnp.concatenate(
                [
                    every(off * lb + at, seq_size, rows)
                    * diag_turned[
                        turn * per_round + off,
                        pl.ds(pl.multiple_of(at * seq_size, seq_size), seq_size),
                    ].astype(F32)
                    for off in range(per_round)
                ],
                axis=0,
            ).astype(BF16)

        def go(pair, carry):
            at = pair * 2
            grads = [grad_of(at), grad_of(at + 1)]
            out[at, turn * span : (turn + 1) * span] = grads[0]
            out[at + 1, turn * span : (turn + 1) * span] = grads[1]
            made = matmul_nt(
                jnp.concatenate(grads, axis=1),
                jnp.concatenate([vals[at], vals[at + 1]], axis=1),
            )
            for c in range(chans):
                r_acc[c] += made[:, c * col : (c + 1) * col]
            return carry

        lax.fori_loop(0, lb // 2, go, 0)
        for c in range(chans):
            for x in range(xs):
                r_send[turn, c % 2 * xs + x, c // 2] = jnp.concatenate(
                    [
                        r_acc[c, pl.ds(off * seq_size + x, yzs, stride=xs), :]
                        for off in range(per_round)
                    ],
                    axis=0,
                ).astype(BF16)
        over_group(r_send.at[turn], r_recv.at[turn], rg_send.at[turn], rg_recv.at[turn])

    def right_rows(turn):
        summed = group_sum(r_recv.at[turn], rg_recv.at[turn])
        for chip in range(2):
            for off in range(per_round):
                r_rows[chip, pl.ds(turn * per_round + off, yzs, stride=lb), :] = summed[
                    chip, off * yzs : (off + 1) * yzs
                ]

    back(0)
    back(1)
    middle = block // 2

    def early_part(at, carry):
        out_acc[at] = matmul(frt[:, :middle], out[at, :middle])
        return carry

    lax.fori_loop(0, lb, early_part, 0)
    back(2)
    over_yz(group_sum(l_recv, lg_recv).reshape(l_ysend.shape), l_ysend, l_yrecv, ly_sems, True)
    drain(p_xrecv.at[pl.ds(0, xs - 1)], px_sems.at[1])
    over_yz(jnp.sum(p_xrecv[...].astype(F32), axis=0), p_ysend, p_yrecv, py_sems, False)
    back(3)

    def late_part(at, carry):
        total = out_acc[at] + matmul(frt[:, middle:], out[at, middle:])
        out[at] = (total * gate[at].astype(F32)).astype(BF16)
        pltpu.make_async_copy(out.at[at], input_grad_hbm.at[at], out_sem).start()
        return carry

    lax.fori_loop(0, lb // 2, late_part, 0)
    for turn in range(ROUNDS):
        right_rows(turn)
    over_yz(r_rows[...].reshape(r_ysend.shape), r_ysend, r_yrecv, ry_sems, True)
    lax.fori_loop(lb // 2, lb, late_part, 0)

    for turn in range(ROUNDS):
        part = pl.ds(turn * per_round, per_round)
        drain(cot.at[mc, part], far_send.at[turn])
        drain(cot.at[mc, part], sib_send.at[turn])
        drain(cot.at[far, part], fwd_send.at[turn])
        drain(send2.at[turn, pl.ds(0, seq_size - 1)], s2_send.at[turn])
        drain(r_send.at[turn, pl.ds(0, 2 * xs - 1)], rg_send.at[turn])
    drain(send1.at[pl.ds(0, seq_size - 1)], s1_send)
    drain(l_send.at[pl.ds(0, 2 * xs - 1)], lg_send)
    drain(p_send.at[pl.ds(0, xs - 1)], px_sems.at[0])
    for sends, sems in ((p_ysend, py_sems), (l_ysend, ly_sems), (r_ysend, ry_sems)):
        drain(sends.at[pl.ds(0, sends.shape[0] - 1)], sems.at[0])
    drain(out, out_sem)
    stores = [
        pltpu.make_async_copy(proj_grad, proj_grad_hbm, small_sem.at[0]),
        pltpu.make_async_copy(left_grad, left_grad_hbm, small_sem.at[1]),
        pltpu.make_async_copy(right_grad, right_grad_hbm, small_sem.at[2]),
    ]
    left_grad[...] = yz_sum(l_yrecv, ly_sems) * scale
    stores[1].start()
    proj_grad[...] = yz_sum(p_yrecv, py_sems) * (1.0 / block)
    stores[0].start()
    right_grad[...] = yz_sum(r_yrecv, ry_sems) * scale
    stores[2].start()
    for store in stores:
        store.wait()


def copy_kernel(*refs):
    srcs, dsts, held, sems = refs[:4], refs[4:8], refs[8:12], refs[12]
    lb = srcs[0].shape[0]
    hops = [(srcs[0].at[at], held[0].at[at], dsts[0].at[at]) for at in range(lb)]
    hops += list(zip(srcs[1:], held[1:], dsts[1:]))
    loads = [pltpu.make_async_copy(a, b, sems.at[0, n]) for n, (a, b, c) in enumerate(hops)]
    stores = [pltpu.make_async_copy(b, c, sems.at[1, n]) for n, (a, b, c) in enumerate(hops)]
    for load in loads:
        load.start()
    for load, store in zip(loads, stores):
        load.wait()
        store.start()
    for store in stores:
        store.wait()


def on_device(activation, gating, kernel_diag, cotangent, factor_right, factor_left, projection):
    row_count, width = activation.shape
    block = factor_right.shape[0]
    lb = row_count // block
    full = projection.shape[1]
    seq_size = lax.axis_size("seq")
    chans = lax.axis_size("chan")
    cube = (lb, block, width)
    share = full // seq_size
    col = block // chans
    xs = min(4, seq_size // 2)
    yzs = seq_size // xs
    dma = pltpu.SemaphoreType.DMA
    per_round = lb // ROUNDS
    span = per_round * seq_size

    def small(*lead):
        return pltpu.VMEM(lead + (lb, col), F32)

    scratch = [
        pltpu.VMEM(cube, BF16),
        pltpu.VMEM(cube, BF16),
        pltpu.VMEM(cube, BF16),
        pltpu.VMEM((chans,) + cube, BF16),
        pltpu.VMEM((block, block), BF16),
        pltpu.VMEM((block, block), BF16),
        pltpu.VMEM((width, full), BF16),
        pltpu.VMEM((block, block), BF16),
        pltpu.VMEM((block, block), BF16),
        pltpu.VMEM(cube, BF16),
        pltpu.VMEM(cube, BF16),
        pltpu.VMEM((seq_size, lb * lb, width), BF16),
        pltpu.VMEM((seq_size, lb * lb, width), BF16),
        pltpu.VMEM(cube, BF16),
        pltpu.VMEM((ROUNDS, seq_size, per_round * lb, width), BF16),
        pltpu.VMEM((seq_size, ROUNDS, per_round * lb, width), BF16),
        pltpu.VMEM((width // LANES, block * lb, LANES), F32),
        pltpu.VMEM(cube, BF16),
        pltpu.VMEM(cube, F32),
        pltpu.VMEM((width, full), F32),
        pltpu.VMEM((xs, yzs, share, width), BF16),
        pltpu.VMEM((xs, yzs, share, width), BF16),
        pltpu.VMEM((yzs, share, width), BF16),
        pltpu.VMEM((yzs, share, width), BF16),
        pltpu.VMEM((block, block), F32),
        pltpu.VMEM((2 * xs, 2, yzs * lb, col), BF16),
        pltpu.VMEM((2 * xs, 2, yzs * lb, col), BF16),
        small(2 * yzs), small(2 * yzs),
        pltpu.VMEM((chans, span, col), F32),
        pltpu.VMEM((ROUNDS, 2 * xs, 2, span // xs, col), BF16),
        pltpu.VMEM((ROUNDS, 2 * xs, 2, span // xs, col), BF16),
        pltpu.VMEM((2, yzs * lb, col), F32),
        small(2 * yzs), small(2 * yzs),
        pltpu.VMEM((share, width), F32), small(), small(),
        dma((7,)), dma, dma((3,)),
    ] + [dma((ROUNDS,))] * 6 + [
        dma, dma, dma((ROUNDS,)), dma((ROUNDS,)), dma((ROUNDS,)), dma((ROUNDS,)), dma, dma,
    ] + [dma((2,))] * 4
    any_space = pl.BlockSpec(memory_space=pl.ANY)
    shapes = [
        jax.ShapeDtypeStruct(cube, BF16),
        jax.ShapeDtypeStruct((share, width), F32),
        jax.ShapeDtypeStruct((lb, col), F32),
        jax.ShapeDtypeStruct((lb, col), F32),
    ]
    results = pl.pallas_call(
        functools.partial(kernel, float((block * full) ** (-0.5))),
        out_shape=shapes,
        in_specs=[any_space] * 7,
        out_specs=[any_space] * 4,
        scratch_shapes=scratch,
        compiler_params=pltpu.CompilerParams(
            collective_id=0, has_side_effects=True, vmem_limit_bytes=58 * 1024 * 1024
        ),
        cost_estimate=pl.CostEstimate(
            flops=20 * row_count * block * width, bytes_accessed=12 * row_count * width,
            transcendentals=0,
        ),
        name="monarch_backward",
    )(
        activation.reshape(cube), gating.reshape(cube), kernel_diag.reshape(cube),
        cotangent.reshape(cube), factor_right, factor_left, projection,
    )
    input_grad, proj_grad, right_grad, left_grad = pl.pallas_call(
        copy_kernel,
        out_shape=shapes,
        in_specs=[any_space] * 4,
        out_specs=[any_space] * 4,
        scratch_shapes=[pltpu.VMEM(shape.shape, shape.dtype) for shape in shapes]
        + [dma((2, lb + 3))],
        name="copy_results",
    )(*results)
    return (input_grad.reshape(row_count, width), proj_grad.T, right_grad, left_grad)


def solution(mesh):
    in_specs = (
        P("seq", "chan"),
        P("seq", "chan"),
        P("seq", "chan"),
        P("seq", "chan"),
        P(),
        P(),
        P("chan", None),
    )
    out_specs = (P("seq", "chan"), P("chan", "seq"), P("seq", "chan"), P("seq", "chan"))
    return jax.shard_map(
        on_device, mesh=mesh, in_specs=in_specs, out_specs=out_specs, check_vma=False
    )
```

```python
import functools

import jax
import jax.numpy as jnp
from jax import lax
from jax.experimental import pallas as pl
from jax.experimental.pallas import tpu as pltpu
from jax.sharding import PartitionSpec as P

ROUNDS = 4
LANES = 128
FIRST_CROSS = 1
SECOND_CROSS = 3
F32 = jnp.float32
BF16 = jnp.bfloat16


def matmul(left, right):
    return jnp.dot(left, right, preferred_element_type=F32)


def matmul_nt(left, right):
    return lax.dot_general(left, right, (((1,), (1,)), ((), ())), preferred_element_type=F32)


def kernel(
    scale,
    act_hbm, gate_hbm, diag_hbm, cot_hbm, right_hbm, left_hbm, proj_hbm,
    input_grad_hbm, proj_grad_hbm, right_grad_hbm, left_grad_hbm,
    act, gate, diag, cot, fr, fl, proj, frt, flt, diag_turned,
    vals, send1, recv1, mg, send2, recv2, staging, out, out_acc,
    p_acc, p_send, p_xrecv, p_ysend, p_yrecv,
    l_acc, l_send, l_recv, l_ysend, l_yrecv,
    r_acc, r_send, r_recv, r_rows, r_ysend, r_yrecv,
    proj_grad, right_grad, left_grad,
    in_sem, out_sem, small_sem,
    far_send, far_recv, sib_send, sib_recv, fwd_send, fwd_recv,
    s1_send, s1_recv, s2_send, s2_recv, rg_send, rg_recv, lg_send, lg_recv,
    px_sems, py_sems, ly_sems, ry_sems,
):
    seq_size = recv1.shape[0]
    lb, block, width = vals.shape
    per_round = lb // ROUNDS
    rows = per_round * lb
    chans = cot.shape[0]
    me = lax.axis_index("seq")
    mc = lax.axis_index("chan")
    sibling = mc + 1 - 2 * lax.rem(mc, 2)
    far = lax.rem(mc + 2, 4)
    far_sibling = 3 - mc
    my_lo = mc // 2
    my_core = lax.rem(mc, 2)
    half = seq_size // 2
    xs = p_send.shape[0]
    zs = half // xs
    yzs = seq_size // xs
    my_half = me // half
    my_z = lax.rem(me, half) // xs
    my_x = lax.rem(me, xs)
    my_yz = me // xs

    barrier = pltpu.get_barrier_semaphore()

    def greet(step, carry):
        other = lax.rem(me + step, seq_size)
        pl.semaphore_signal(
            barrier, inc=1, device_id=(other, mc), device_id_type=pl.DeviceIdType.MESH
        )
        return carry

    group = [
        (lax.rem(my_x + x_off, xs), chan)
        for x_off in range(xs)
        for chan in (mc, sibling)
        if x_off > 0 or chan is not mc
    ]
    for x, chan in group:
        if chan is not mc:
            pl.semaphore_signal(
                barrier, inc=1, device_id=(my_yz * xs + x, chan),
                device_id_type=pl.DeviceIdType.MESH,
            )

    def greet_far(step, carry):
        other = lax.rem(my_yz + step, yzs) * xs + my_x
        pl.semaphore_signal(
            barrier, inc=1, device_id=(other, far), device_id_type=pl.DeviceIdType.MESH
        )
        return carry

    lax.fori_loop(0, yzs, greet_far, 0)
    lax.fori_loop(1, seq_size, greet, 0)

    loads = [
        pltpu.make_async_copy(src, dst, in_sem.at[at])
        for at, (src, dst) in enumerate(
            (
                (act_hbm, act),
                (gate_hbm, gate),
                (right_hbm, fr),
                (diag_hbm, diag),
                (cot_hbm, cot.at[mc]),
                (proj_hbm, proj),
                (left_hbm, fl),
            )
        )
    ]
    for load in loads:
        load.start()

    def send(src, dst, send_sem, recv_sem, device):
        return pltpu.make_async_remote_copy(
            src_ref=src, dst_ref=dst, send_sem=send_sem, recv_sem=recv_sem,
            device_id=device, device_id_type=pl.DeviceIdType.MESH,
        )

    def drain(ref, sem):
        pltpu.make_async_copy(ref, ref, sem).wait()

    def place(step, cross):
        turn = lax.rem(step, zs)
        z_off = (2 * lax.rem(turn, 2) - 1) * ((turn + 1) // 2)
        x_off = step // zs
        z = lax.rem(my_z + z_off + zs, zs)
        x = lax.rem(my_x + x_off, xs)
        return lax.rem(my_half + cross, 2) * half + z * xs + x

    def first_sends(cross, first, count):
        part = pl.ds(first * lb, count * lb)

        def go(step, carry):
            other = place(step, cross)
            send(
                send1.at[other, part], recv1.at[me, part], s1_send, s1_recv, (other, mc)
            ).start()
            return carry

        lax.fori_loop(1 - cross, half, go, 0)

    def second_sends(turn, cross):
        def go(step, carry):
            other = place(step, cross)
            send(
                send2.at[turn, other], recv2.at[me, turn], s2_send.at[turn], s2_recv.at[turn],
                (other, mc),
            ).start()
            return carry

        lax.fori_loop(1 - cross, half, go, 0)

    for load in loads[:4]:
        load.wait()

    for pair in range(lb // 2):
        pieces = []
        for at in (2 * pair, 2 * pair + 1):
            value = (act[at].astype(F32) * gate[at].astype(F32)).astype(BF16)
            vals[at] = value
            made = matmul(fr[...], value) * diag[at].astype(F32)
            pieces.append(made.reshape(seq_size, lb, width))
        send1[:, 2 * pair * lb : (2 * pair + 2) * lb, :] = jnp.concatenate(
            pieces, axis=1
        ).astype(BF16)
        if pair == 0:
            pl.semaphore_wait(barrier, seq_size - 1 + xs + yzs)
            for turn in range(ROUNDS):
                part = pl.ds(turn * per_round, per_round)
                send(
                    cot_hbm.at[part], cot.at[mc, part], far_send.at[turn], far_recv.at[turn], (me, far)
                ).start()
            for turn in range(ROUNDS):
                part = pl.ds(turn * per_round, per_round)
                send(
                    cot_hbm.at[part], cot.at[mc, part], sib_send.at[turn], sib_recv.at[turn],
                    (me, sibling),
                ).start()
        first_sends(0, 2 * pair, 2)
    recv1[me] = send1[me]

    for load in loads[4:]:
        load.wait()
    flt[...] = fl[...].T

    def stage(blocks):
        count = blocks.shape[0] * blocks.shape[1]
        flat = blocks.reshape(count, width).astype(F32)
        for part in range(width // LANES):
            staging[part, :count] = flat[:, part * LANES : (part + 1) * LANES]

    def every(start, count, stride):
        return jnp.concatenate(
            [
                staging[part, pl.ds(start, count, stride=stride), :]
                for part in range(width // LANES)
            ],
            axis=1,
        )

    for col in range(block // LANES):
        staging[0, col * block : (col + 1) * block] = fr[
            :, col * LANES : (col + 1) * LANES
        ].astype(F32)
    for kk in range(lb):
        turned = jnp.concatenate(
            [
                staging[0, pl.ds(col * block + kk, seq_size, stride=lb), :]
                for col in range(block // LANES)
            ],
            axis=1,
        )
        frt[:, kk * seq_size : (kk + 1) * seq_size] = turned.T.astype(BF16)
    stage(diag[...])

    def turn_diag(kk, carry):
        diag_turned[kk] = every(kk, block, lb).astype(BF16)
        return carry

    lax.fori_loop(0, lb, turn_diag, 0)

    for turn in range(ROUNDS):
        part = pl.ds(turn * per_round, per_round)
        drain(cot.at[far, part], far_recv.at[turn])
        forward = send(
            cot.at[far, part], cot.at[far, part], fwd_send.at[turn], fwd_recv.at[turn],
            (me, sibling),
        )
        forward.start()
        if turn == SECOND_CROSS:
            for earlier in range(turn):
                second_sends(earlier, 1)
        drain(cot.at[sibling, part], sib_recv.at[turn])
        drain(cot.at[far_sibling, part], fwd_recv.at[turn])
        pieces = []
        for off in range(per_round):
            at = turn * per_round + off
            total = matmul_nt(cot[0, at], proj[:, :width])
            for c in range(1, chans):
                total += matmul_nt(cot[c, at], proj[:, c * width : (c + 1) * width])
            up = total.astype(BF16)
            mg[at] = up
            pieces.append(matmul(flt[...], up).reshape(seq_size, lb, width))
        send2[turn] = jnp.concatenate(pieces, axis=1).astype(BF16)
        if turn >= SECOND_CROSS:
            second_sends(turn, 1)
        second_sends(turn, 0)
        recv2[me, turn] = send2[turn, me]
        if turn == FIRST_CROSS:
            first_sends(1, 0, lb)

    drain(recv1.at[pl.ds(0, seq_size - 1)], s1_recv)
    stage(recv1[...])
    p_acc[...] = jnp.zeros_like(p_acc)
    l_acc[...] = jnp.zeros_like(l_acc)

    def mixed_part(pair, carry):
        at = pair * 2
        got = jnp.concatenate([every(at, block, lb), every(at + 1, block, lb)], axis=1)
        got = got.astype(BF16)
        l_acc[...] += matmul_nt(jnp.concatenate([mg[at], mg[at + 1]], axis=1), got)
        mixed = matmul(fl[...], got).astype(BF16)
        turned = jnp.concatenate([mixed[:, :width].T, mixed[:, width:].T], axis=1)
        for c in range(chans):
            p_acc[:, c * width : (c + 1) * width] += matmul(
                turned, cot[c, pl.ds(at, 2)].reshape(2 * block, width)
            )
        return carry

    lax.fori_loop(0, lb // 2, mixed_part, 0)

    def over_group(sends, recvs, ssem, rsem):
        mine = my_core * xs + my_x
        for x, chan in group:
            send(
                sends.at[lax.rem(chan, 2) * xs + x], recvs.at[mine], ssem, rsem,
                (my_yz * xs + x, chan),
            ).start()
        recvs[mine] = sends[mine]

    def group_sum(recvs, rsem):
        drain(recvs.at[pl.ds(0, 2 * xs - 1)], rsem)
        return jnp.sum(recvs[...].astype(F32), axis=0)

    def over_yz(total, sends, recvs, sems, pair):
        sends[...] = total.astype(sends.dtype)
        near = my_lo * yzs if pair else 0

        def go(first, chan):
            def step_to(step, carry):
                other = lax.rem(my_yz + step, yzs)
                send(
                    sends.at[first + other], recvs.at[near + my_yz], sems.at[0], sems.at[1],
                    (other * xs + my_x, chan),
                ).start()
                return carry

            return step_to

        if pair:
            lax.fori_loop(0, yzs, go((1 - my_lo) * yzs, far), 0)
        lax.fori_loop(1, yzs, go(near, mc), 0)
        recvs[near + my_yz] = sends[near + my_yz]

    def yz_sum(recvs, sems):
        drain(recvs.at[pl.ds(0, recvs.shape[0] - 1)], sems.at[1])
        return jnp.sum(recvs[...].astype(F32), axis=0)

    col = block // chans
    split = l_acc[...].reshape(yzs, xs, lb, block)
    for c in range(chans):
        for x in range(xs):
            l_send[c % 2 * xs + x, c // 2] = (
                split[:, x, :, c * col : (c + 1) * col].reshape(yzs * lb, col).astype(BF16)
            )
    over_group(l_send, l_recv, lg_send, lg_recv)
    share = p_send.shape[2]
    per_chan = yzs // chans
    for c in range(chans):
        turned = p_acc[:, c * width : (c + 1) * width].T.astype(BF16)
        turned = turned.reshape(per_chan, xs, share, width)
        for x in range(xs):
            p_send[x, c * per_chan : (c + 1) * per_chan] = turned[:, x]
    for x_off in range(1, xs):
        x = lax.rem(my_x + x_off, xs)
        send(
            p_send.at[x], p_xrecv.at[my_x], px_sems.at[0], px_sems.at[1], (my_yz * xs + x, mc)
        ).start()
    p_xrecv[my_x] = p_send[my_x]

    def back(turn):
        drain(recv2.at[pl.ds(0, seq_size - 1), turn], s2_recv.at[turn])
        stage(recv2[:, turn])
        r_acc[...] = jnp.zeros_like(r_acc)
        span = per_round * seq_size

        def grad_of(at):
            return jnp.concatenate(
                [
                    every(off * lb + at, seq_size, rows)
                    * diag_turned[
                        turn * per_round + off,
                        pl.ds(pl.multiple_of(at * seq_size, seq_size), seq_size),
                    ].astype(F32)
                    for off in range(per_round)
                ],
                axis=0,
            ).astype(BF16)

        def go(pair, carry):
            at = pair * 2
            grads = [grad_of(at), grad_of(at + 1)]
            out[at, turn * span : (turn + 1) * span] = grads[0]
            out[at + 1, turn * span : (turn + 1) * span] = grads[1]
            made = matmul_nt(
                jnp.concatenate(grads, axis=1),
                jnp.concatenate([vals[at], vals[at + 1]], axis=1),
            )
            for c in range(chans):
                r_acc[c] += made[:, c * col : (c + 1) * col]
            return carry

        lax.fori_loop(0, lb // 2, go, 0)
        for c in range(chans):
            for x in range(xs):
                r_send[turn, c % 2 * xs + x, c // 2] = jnp.concatenate(
                    [
                        r_acc[c, pl.ds(off * seq_size + x, yzs, stride=xs), :]
                        for off in range(per_round)
                    ],
                    axis=0,
                ).astype(BF16)
        over_group(r_send.at[turn], r_recv.at[turn], rg_send.at[turn], rg_recv.at[turn])

    def right_rows(turn):
        summed = group_sum(r_recv.at[turn], rg_recv.at[turn])
        for chip in range(2):
            for off in range(per_round):
                r_rows[chip, pl.ds(turn * per_round + off, yzs, stride=lb), :] = summed[
                    chip, off * yzs : (off + 1) * yzs
                ]

    back(0)
    back(1)
    middle = block // 2

    def early_part(at, carry):
        out_acc[at] = matmul(frt[:, :middle], out[at, :middle])
        return carry

    lax.fori_loop(0, lb, early_part, 0)
    back(2)
    over_yz(group_sum(l_recv, lg_recv).reshape(l_ysend.shape), l_ysend, l_yrecv, ly_sems, True)
    drain(p_xrecv.at[pl.ds(0, xs - 1)], px_sems.at[1])
    over_yz(jnp.sum(p_xrecv[...].astype(F32), axis=0), p_ysend, p_yrecv, py_sems, False)
    back(3)

    def late_part(at, carry):
        total = out_acc[at] + matmul(frt[:, middle:], out[at, middle:])
        out[at] = (total * gate[at].astype(F32)).astype(BF16)
        pltpu.make_async_copy(out.at[at], input_grad_hbm.at[at], out_sem).start()
        return carry

    lax.fori_loop(0, lb // 2, late_part, 0)
    for turn in range(ROUNDS):
        right_rows(turn)
    over_yz(r_rows[...].reshape(r_ysend.shape), r_ysend, r_yrecv, ry_sems, True)
    lax.fori_loop(lb // 2, lb, late_part, 0)

    for turn in range(ROUNDS):
        part = pl.ds(turn * per_round, per_round)
        drain(cot.at[mc, part], far_send.at[turn])
        drain(cot.at[mc, part], sib_send.at[turn])
        drain(cot.at[far, part], fwd_send.at[turn])
        drain(send2.at[turn, pl.ds(0, seq_size - 1)], s2_send.at[turn])
        drain(r_send.at[turn, pl.ds(0, 2 * xs - 1)], rg_send.at[turn])
    drain(send1.at[pl.ds(0, seq_size - 1)], s1_send)
    drain(l_send.at[pl.ds(0, 2 * xs - 1)], lg_send)
    drain(p_send.at[pl.ds(0, xs - 1)], px_sems.at[0])
    for sends, sems in ((p_ysend, py_sems), (l_ysend, ly_sems), (r_ysend, ry_sems)):
        drain(sends.at[pl.ds(0, sends.shape[0] - 1)], sems.at[0])
    drain(out, out_sem)
    stores = [
        pltpu.make_async_copy(proj_grad, proj_grad_hbm, small_sem.at[0]),
        pltpu.make_async_copy(left_grad, left_grad_hbm, small_sem.at[1]),
        pltpu.make_async_copy(right_grad, right_grad_hbm, small_sem.at[2]),
    ]
    left_grad[...] = yz_sum(l_yrecv, ly_sems) * scale
    stores[1].start()
    proj_grad[...] = yz_sum(p_yrecv, py_sems) * (1.0 / block)
    stores[0].start()
    right_grad[...] = yz_sum(r_yrecv, ry_sems) * scale
    stores[2].start()
    for store in stores:
        store.wait()


def copy_kernel(*refs):
    srcs, dsts, held, sems = refs[:4], refs[4:8], refs[8:12], refs[12]
    lb = srcs[0].shape[0]
    hops = [(srcs[0].at[at], held[0].at[at], dsts[0].at[at]) for at in range(lb)]
    hops += list(zip(srcs[1:], held[1:], dsts[1:]))
    loads = [pltpu.make_async_copy(a, b, sems.at[0, n]) for n, (a, b, c) in enumerate(hops)]
    stores = [pltpu.make_async_copy(b, c, sems.at[1, n]) for n, (a, b, c) in enumerate(hops)]
    for load in loads:
        load.start()
    for load, store in zip(loads, stores):
        load.wait()
        store.start()
    for store in stores:
        store.wait()


def on_device(activation, gating, kernel_diag, cotangent, factor_right, factor_left, projection):
    row_count, width = activation.shape
    block = factor_right.shape[0]
    lb = row_count // block
    full = projection.shape[1]
    seq_size = lax.axis_size("seq")
    chans = lax.axis_size("chan")
    cube = (lb, block, width)
    share = full // seq_size
    col = block // chans
    xs = min(4, seq_size // 2)
    yzs = seq_size // xs
    dma = pltpu.SemaphoreType.DMA
    per_round = lb // ROUNDS
    span = per_round * seq_size

    def small(*lead):
        return pltpu.VMEM(lead + (lb, col), F32)

    scratch = [
        pltpu.VMEM(cube, BF16),
        pltpu.VMEM(cube, BF16),
        pltpu.VMEM(cube, BF16),
        pltpu.VMEM((chans,) + cube, BF16),
        pltpu.VMEM((block, block), BF16),
        pltpu.VMEM((block, block), BF16),
        pltpu.VMEM((width, full), BF16),
        pltpu.VMEM((block, block), BF16),
        pltpu.VMEM((block, block), BF16),
        pltpu.VMEM(cube, BF16),
        pltpu.VMEM(cube, BF16),
        pltpu.VMEM((seq_size, lb * lb, width), BF16),
        pltpu.VMEM((seq_size, lb * lb, width), BF16),
        pltpu.VMEM(cube, BF16),
        pltpu.VMEM((ROUNDS, seq_size, per_round * lb, width), BF16),
        pltpu.VMEM((seq_size, ROUNDS, per_round * lb, width), BF16),
        pltpu.VMEM((width // LANES, block * lb, LANES), F32),
        pltpu.VMEM(cube, BF16),
        pltpu.VMEM(cube, F32),
        pltpu.VMEM((width, full), F32),
        pltpu.VMEM((xs, yzs, share, width), BF16),
        pltpu.VMEM((xs, yzs, share, width), BF16),
        pltpu.VMEM((yzs, share, width), BF16),
        pltpu.VMEM((yzs, share, width), BF16),
        pltpu.VMEM((block, block), F32),
        pltpu.VMEM((2 * xs, 2, yzs * lb, col), BF16),
        pltpu.VMEM((2 * xs, 2, yzs * lb, col), BF16),
        small(2 * yzs), small(2 * yzs),
        pltpu.VMEM((chans, span, col), F32),
        pltpu.VMEM((ROUNDS, 2 * xs, 2, span // xs, col), BF16),
        pltpu.VMEM((ROUNDS, 2 * xs, 2, span // xs, col), BF16),
        pltpu.VMEM((2, yzs * lb, col), F32),
        small(2 * yzs), small(2 * yzs),
        pltpu.VMEM((share, width), F32), small(), small(),
        dma((7,)), dma, dma((3,)),
    ] + [dma((ROUNDS,))] * 6 + [
        dma, dma, dma((ROUNDS,)), dma((ROUNDS,)), dma((ROUNDS,)), dma((ROUNDS,)), dma, dma,
    ] + [dma((2,))] * 4
    any_space = pl.BlockSpec(memory_space=pl.ANY)
    shapes = [
        jax.ShapeDtypeStruct(cube, BF16),
        jax.ShapeDtypeStruct((share, width), F32),
        jax.ShapeDtypeStruct((lb, col), F32),
        jax.ShapeDtypeStruct((lb, col), F32),
    ]
    results = pl.pallas_call(
        functools.partial(kernel, float((block * full) ** (-0.5))),
        out_shape=shapes,
        in_specs=[any_space] * 7,
        out_specs=[any_space] * 4,
        scratch_shapes=scratch,
        compiler_params=pltpu.CompilerParams(
            collective_id=0, has_side_effects=True, vmem_limit_bytes=58 * 1024 * 1024
        ),
        cost_estimate=pl.CostEstimate(
            flops=20 * row_count * block * width, bytes_accessed=12 * row_count * width,
            transcendentals=0,
        ),
        name="monarch_backward",
    )(
        activation.reshape(cube), gating.reshape(cube), kernel_diag.reshape(cube),
        cotangent.reshape(cube), factor_right, factor_left, projection,
    )
    input_grad, proj_grad, right_grad, left_grad = pl.pallas_call(
        copy_kernel,
        out_shape=shapes,
        in_specs=[any_space] * 4,
        out_specs=[any_space] * 4,
        scratch_shapes=[pltpu.VMEM(shape.shape, shape.dtype) for shape in shapes]
        + [dma((2, lb + 3))],
        name="copy_results",
    )(*results)
    return (input_grad.reshape(row_count, width), proj_grad.T, right_grad, left_grad)


def solution(mesh):
    in_specs = (
        P("seq", "chan"),
        P("seq", "chan"),
        P("seq", "chan"),
        P("seq", "chan"),
        P(),
        P(),
        P("chan", None),
    )
    out_specs = (P("seq", "chan"), P("chan", "seq"), P("seq", "chan"), P("seq", "chan"))
    return jax.shard_map(
        on_device, mesh=mesh, in_specs=in_specs, out_specs=out_specs, check_vma=False
    )
```
